256 devices in a mesh: seq: 2 (over core), fsdp: 128 (over x, z, y).
Axes of the slice: x: 4, y: 4, z: 8, core: 2. Of those that a mesh axis runs over, the one named last changes fastest.
Arguments:
- hidden: bfloat16 [128, 512, 768], P('fsdp', 'seq'), may hold values from -24 to 24
- d_out: bfloat16 [128, 512, 768], P('fsdp', 'seq'), may hold values from -24 to 24
- lengths: int32 [128, 2], P('fsdp'), may hold values from 1 to 12, 16 in all within a row
- slot_source: int32 [128, 512], P('fsdp'), may hold values from 0 to 511, each once within a row
- first_gain: bfloat16 [768], P('fsdp'), may hold values from 0.099609375 to 1.8984375
- qkv_weight: bfloat16 [768, 2304], P('fsdp'), may hold values from -0.21875 to 0.21875
- out_weight: bfloat16 [768, 768], P(None, 'fsdp'), may hold values from -2 to 2
- second_gain: bfloat16 [768], P('fsdp'), may hold values from 0.099609375 to 1.8984375
- up_weight: bfloat16 [768, 3072], P('fsdp'), may hold values from -0.21875 to 0.21875
- up_bias: bfloat16 [3072], P('fsdp'), may hold values from -3 to 3
- down_weight: bfloat16 [3072, 768], P(None, 'fsdp'), may hold values from -0.109375 to 0.109375
- down_bias: bfloat16 [768], P('fsdp'), may hold values from -3 to 3
Outputs:
- output: bfloat16 [128, 512, 768], P('fsdp', 'seq')
- grad_hidden: float32 [128, 512, 768], P('fsdp', 'seq')
- grad_first_gain: float32 [768], P('fsdp')
- grad_qkv: float32 [768, 2304], P('fsdp')
- grad_out: float32 [768, 768], P(None, 'fsdp')
- grad_second_gain: float32 [768], P('fsdp')
- grad_up: float32 [768, 3072], P('fsdp')
- grad_up_bias: float32 [3072], P('fsdp')
- grad_down: float32 [3072, 768], P(None, 'fsdp')
- grad_down_bias: float32 [768], P('fsdp')
The draws below stay inside these ranges and needn't reach their ends.
Inputs may be any that keep to these rules, and one draw needn't show every extreme that they name: `lengths`: each row lists whole sequences in blocks of 16 tokens; it sums to 16 and no entry exceeds 12. `slot_source`: each row is a permutation of the group's rows.
All inputs are finite; a program needn't handle non-finite values.
Results may differ from the reference program's by a relative error of at most 0.017.
Values may be sent and summed in bfloat16 or wider, within the bound.
A program may use at most 192 MiB of HBM per device.

```python
import math
import jax
import jax.numpy as jnp
import numpy as np
from jax import lax

D = 768
HEADS = 12
HD = 64
FF = 3072
BLOCK = 16
SEQS = 2
CLEAN = 256
MOST_BLK = 12
PACK = 512
GROUPS = 128


def with_spikes(values, key, source, target, shards_of, factor):
    def block_of(dim):
        return (jnp.arange(values.shape[dim]) // (values.shape[dim] // shards_of)).reshape((-1,) + (1,) * (values.ndim - 1 - dim))

    near = jax.random.permutation(key, shards_of)[block_of(target)]
    other_side = (block_of(target) + shards_of // 2) % shards_of
    return jnp.where((block_of(source) == near) | (block_of(source) == other_side), factor * values, values)


def shard_levels(own_key, shape, cuts, least, largest):
    gain = 1.0
    for dim, shards_of in cuts:
        heights = jax.random.uniform(jax.random.fold_in(jax.random.fold_in(own_key, 6), dim), (shards_of,), jnp.float32, least / len(cuts), largest / len(cuts))
        gain = gain * jnp.repeat(jnp.exp(heights), shape[dim] // shards_of).reshape((-1,) + (1,) * (len(shape) - 1 - dim))
    return gain


def split_up(number_of, total, limit, skew):
    loads = [(1 << 20) // math.isqrt(rank ** skew) + 1 for rank in range(2, number_of + 1)]
    rest, given = total - limit - (number_of - 1), [1] * (number_of - 1)
    while rest > 0:
        candidates = [i for i in range(number_of - 1) if given[i] < limit]
        whole, remaining = sum([loads[i] for i in candidates]), rest
        for i in candidates:
            addition = min(limit - given[i], max(1, remaining * loads[i] // whole), rest)
            given[i] = given[i] + addition
            rest = rest - addition
    return np.array([limit] + given)


def ragged_sizes(rng, number_of, total, limit, skew):
    if number_of == 2:
        one = jax.random.randint(rng, (), max(1, total - limit), min(limit, total - 1) + 1)
        return jnp.stack([one, total - one])
    tallies = jnp.asarray(split_up(number_of, total, limit, skew), jnp.int32)
    couples = (number_of - 1) // 2
    donor, receiver = tallies[1:1 + 2 * couples:2], tallies[2:2 + 2 * couples:2]
    margin = jnp.minimum(donor - 1, limit - receiver)
    shifted = jax.random.randint(jax.random.fold_in(rng, 1), (couples,), 0, 1 << 20) % (margin + 1)
    tallies = tallies.at[1:1 + 2 * couples:2].set(donor - shifted).at[2:2 + 2 * couples:2].set(receiver + shifted)
    return tallies[jax.random.permutation(jax.random.fold_in(rng, 2), number_of)]


def bell_draw(own_key, extent, width, reach, split=(), kind=jnp.bfloat16):
    loudness = shard_levels(own_key, extent, split, -0.22, 0.18) if split else 1.0
    values = jax.random.normal(own_key, extent, jnp.float32) * width * loudness
    return jnp.minimum(jnp.maximum(values, -reach), reach).astype(kind)


def gaussian_with(stream_key, dims, spread, bound, cuts, heavy, kind=jnp.bfloat16):
    values = spread * jax.random.normal(stream_key, dims, jnp.float32)
    if cuts:
        values = values * shard_levels(stream_key, dims, cuts, -0.22, 0.18)
    return jnp.clip(with_spikes(values, jax.random.fold_in(stream_key, 3), *heavy), -bound, bound).astype(kind)


def setup_inputs(seed: int = 0) -> dict:
    key_of = jax.random.split(jax.random.key(seed), 13)
    return {
        "hidden": gaussian_with(key_of[0], (GROUPS, PACK, D), 1.0, 24.0, ((0, 128), (1, 2)), (0, 2, 128, 5.5)),
        "d_out": gaussian_with(key_of[1], (GROUPS, PACK, D), 1.0, 24.0, ((0, 128), (1, 2)), (0, 2, 128, 5.5)),
        "lengths": jax.vmap(lambda own: ragged_sizes(own, SEQS, CLEAN // BLOCK, MOST_BLK, 2))(jax.random.split(key_of[2], GROUPS)).reshape((GROUPS, SEQS)).astype(jnp.int32),
        "slot_source": jax.vmap(lambda own: jax.random.permutation(own, PACK))(jax.random.split(key_of[3], GROUPS)).reshape((GROUPS, PACK)).astype(jnp.int32),
        "first_gain": jnp.clip(1.0 + 0.18 * jax.random.normal(key_of[4], (D,), jnp.float32), 0.099609375, 1.8984375).astype(jnp.bfloat16),
        "qkv_weight": bell_draw(key_of[5], (D, 3 * D), D ** -0.5, 0.21875, ((0, 128),)),
        "out_weight": bell_draw(key_of[6], (D, D), (max(D // 96, 1)) ** -0.5, 2.0, ((1, 128),)),
        "second_gain": jnp.clip(1.0 + 0.18 * jax.random.normal(key_of[7], (D,), jnp.float32), 0.099609375, 1.8984375).astype(jnp.bfloat16),
        "up_weight": bell_draw(key_of[8], (D, FF), D ** -0.5, 0.21875, ((0, 128),)),
        "up_bias": bell_draw(key_of[9], (FF,), 0.5, 3.0, ((0, 128),)),
        "down_weight": bell_draw(key_of[10], (FF, D), FF ** -0.5, 0.109375, ((1, 128),)),
        "down_bias": bell_draw(key_of[11], (D,), 0.5, 3.0, ((0, 128),)),
    }


@jax.custom_vjp
def low(v):
    return lax.optimization_barrier(v.astype(jnp.bfloat16)).astype(jnp.float32)

@jax.custom_vjp
def low_back(v):
    return v

def low_keep(v):
    return (low(v), None)

def low_pass(kept, grad):
    return (grad,)

def back_keep(v):
    return (v, None)

def back_low(kept, grad):
    return (low(grad),)
low.defvjp(low_keep, low_pass)
low_back.defvjp(back_keep, back_low)
EPS = 1e-05
NEG = -1e+30
HIGH = lax.Precision.HIGHEST

def normalize(values):
    row_mean = lax.optimization_barrier(jnp.mean(values, axis=-1, keepdims=True))
    centered = values - row_mean
    variance = lax.optimization_barrier(jnp.mean(centered * centered, axis=-1, keepdims=True))
    return centered * lax.rsqrt(variance + EPS)

def token_tables(lengths_row):
    blocks = (jnp.arange(CLEAN, dtype=jnp.int32) // BLOCK).astype(jnp.int32)
    starts = (jnp.cumsum(lengths_row) - lengths_row).astype(jnp.int32)
    begins = lax.optimization_barrier(jnp.max(jnp.where(starts[None, :] <= blocks[:, None], starts[None, :], 0), axis=1)).astype(jnp.int32)
    segment = lax.optimization_barrier(jnp.sum((starts[None, 1:] <= blocks[:, None]).astype(jnp.int32), axis=1)).astype(jnp.int32)
    position = (jnp.arange(CLEAN, dtype=jnp.int32) - BLOCK * begins).astype(jnp.float32)
    frequency = jnp.power(10000.0, -2.0 * jnp.arange(HD // 2, dtype=jnp.float32) / HD)
    angles = position[:, None] * frequency[None, :]
    return (jnp.cos(angles), jnp.sin(angles), segment, blocks)

def rotate(values, cosine, sine):
    half = values.shape[-1] // 2
    first = values[..., :half]
    second = values[..., half:]
    return jnp.concatenate([first * cosine - second * sine, first * sine + second * cosine], axis=-1)

def allowed(segment, blocks):
    slot_seg = jnp.concatenate([segment, segment])
    slot_blk = jnp.concatenate([blocks, blocks])
    slot_noisy = jnp.arange(2 * CLEAN) < CLEAN
    same_segment = slot_seg[:, None] == slot_seg[None, :]
    query_blk = slot_blk[:, None]
    key_blk = slot_blk[None, :]
    query_noisy = slot_noisy[:, None]
    key_noisy = slot_noisy[None, :]
    block_rule = query_noisy & key_noisy & (key_blk == query_blk) | query_noisy & ~key_noisy & (key_blk < query_blk) | ~query_noisy & ~key_noisy & (key_blk <= query_blk)
    return same_segment & block_rule

def block_layer(values, lengths_row, seq_order, params):
    gain_one, qkv_mat, out_mat, gain_two, up_mat, up_vec, down_mat, down_vec = params
    pack_rows = values.shape[0]
    ln_one = low(normalize(values) * gain_one)
    qkv = low_back(low(jnp.dot(ln_one, qkv_mat, precision=HIGH)))
    ordered = jnp.take(qkv, seq_order, axis=0)
    queries = ordered[:, :D].reshape(pack_rows, HEADS, HD)
    keys_all = ordered[:, D:2 * D].reshape(pack_rows, HEADS, HD)
    values_seq = ordered[:, 2 * D:].reshape(pack_rows, HEADS, HD)
    cosine, sine, segment, blocks = token_tables(lengths_row)
    cos_slot = jnp.concatenate([cosine, cosine])[:, None, :]
    sin_slot = jnp.concatenate([sine, sine])[:, None, :]
    rot_queries = low(rotate(queries, cos_slot, sin_slot))
    rot_keys = low(rotate(keys_all, cos_slot, sin_slot))
    scores = low_back(jnp.einsum('qhd,khd->hqk', rot_queries, rot_keys, precision=HIGH) * HD ** (-0.5))
    scores = jnp.where(allowed(segment, blocks)[None], scores, NEG)
    row_max = lax.optimization_barrier(jnp.max(scores, axis=-1, keepdims=True))
    exps = jnp.exp(scores - row_max)
    probs = exps / lax.optimization_barrier(jnp.sum(exps, axis=-1, keepdims=True))
    attention = jnp.einsum('hqk,khd->qhd', low(probs), values_seq, precision=HIGH).reshape(pack_rows, D)
    attention = low_back(low(attention))
    attention = jnp.zeros_like(attention).at[seq_order].set(attention)
    middle = values + low_back(jnp.dot(attention, out_mat, precision=HIGH))
    ln_two = low(normalize(middle) * gain_two)
    pre_act = low_back(jnp.dot(ln_two, up_mat, precision=HIGH) + up_vec)
    act = low(jax.nn.gelu(pre_act, approximate=True))
    return middle + jnp.dot(act, down_mat, precision=HIGH) + down_vec

def reference(hidden, d_out, lengths, slot_source, first_gain, qkv_weight, out_weight, second_gain, up_weight, up_bias, down_weight, down_bias):
    params = tuple((member.astype(jnp.float32) for member in (first_gain, qkv_weight, out_weight, second_gain, up_weight, up_bias, down_weight, down_bias)))
    inputs = hidden.astype(jnp.float32)

    def forward(inputs, params):

        def single(sample):
            return block_layer(sample[0], sample[1], sample[2], params)
        return lax.map(jax.checkpoint(single), (inputs, lengths, slot_source))
    result, pullback = jax.vjp(forward, inputs, params)
    grad_in, gradients = pullback(d_out.astype(jnp.float32))
    return (result.astype(jnp.bfloat16), grad_in, gradients[0], gradients[1], gradients[2], gradients[3], gradients[4], gradients[5], gradients[6], gradients[7])
```

```python
import jax
import jax.numpy as jnp
import numpy as np
from jax import lax
from jax.experimental import pallas as pl
from jax.experimental.pallas import tpu as pltpu
from jax.sharding import PartitionSpec as P

MESH = pl.DeviceIdType.MESH
BF = jnp.bfloat16
F32 = jnp.float32
EPS = 1e-05
NEG = -1e30

NT = 37
VEC, QKV, OUT, UP, DOWN = 0, list(range(1, 10)), [10, 11, 12], list(range(13, 25)), list(range(25, 37))
GVEC, GQKV, GOUT, GUP, GDOWN = 24, list(range(28, 37)), [25, 26, 27], list(range(12, 24)), list(range(12))


class Split:
    def __init__(self, ny, nx, nz, direct_z, direct_x, direct_wide):
        self.ny, self.nx, self.nz = ny, nx, nz
        self.direct_z, self.direct_x, self.direct_wide = direct_z, direct_x, direct_wide
        self.stages = range(len(ny))
        self.first = [sum(4 * ny[i] + nx[i] + nz[i] for i in range(st)) for st in self.stages]
        self.slab = [ny[i] + nx[i] + nz[i] for i in self.stages]

    def x(self, st):
        a = self.first[st] + 4 * self.ny[st]
        return a, a + self.nx[st]

    def z(self, st):
        a = self.first[st] + 4 * self.ny[st] + self.nx[st]
        return a, a + self.nz[st]

    def y(self, st, j):
        return pl.ds(self.first[st] + j * self.ny[st], self.ny[st])

    def tile(self, st, i, y):
        if i < self.ny[st]:
            return self.first[st] + y * self.ny[st] + i
        return self.first[st] + 3 * self.ny[st] + i


GATHER = Split((1, 2), (5, 8), (4, 8), (0, 0), (1, 1), (0, 0))
REDUCE = Split((2, 1), (9, 4), (8, 4), (0, 0), (1, 1), (0, 0))


class Place:
    pass


def chip(x, z, y):
    return x * 32 + z * 4 + y


def place():
    c = Place()
    c.f = lax.axis_index("fsdp")
    c.s = lax.axis_index("seq")
    c.x = c.f // 32
    c.z = (c.f // 4) % 8
    c.y = c.f % 4
    c.zh = c.z // 2
    c.zl = c.z % 2
    c.m = c.f % 8
    sgn = 2 * c.zl - 1
    c.xr = chip((c.x + 1) % 4, c.z, c.y)
    c.xl = chip((c.x + 3) % 4, c.z, c.y)
    c.xo = chip((c.x + 2) % 4, c.z, c.y)
    c.yo = chip(c.x, c.z, (c.y + 2) % 4)
    c.yr = chip(c.x, c.z, (c.y + 1) % 4)
    c.yl = chip(c.x, c.z, (c.y + 3) % 4)
    c.zo = chip(c.x, (c.z + 8 + sgn) % 8, c.y)
    c.zi = chip(c.x, (c.z + 8 - sgn) % 8, c.y)
    c.z2 = chip(c.x, (c.z + 8 + 2 * sgn) % 8, c.y)
    c.z2i = chip(c.x, (c.z + 8 - 2 * sgn) % 8, c.y)
    c.z3 = chip(c.x, (c.z + 8 + 3 * sgn) % 8, c.y)
    c.ke = (c.zh + 4 + sgn) % 4
    c.kf = (c.zh + 4 - sgn) % 4
    c.kp = (c.zh + 2) % 4
    return c


def greet(c):
    sem = pltpu.get_barrier_semaphore()
    group = [c.f - c.m + (c.m + d) % 8 for d in range(1, 8)]
    devices = [c.xr, c.xl, c.xo, c.zo, c.z2, c.z2i, c.z3] + group
    for d in devices:
        pl.semaphore_signal(sem, inc=1, device_id={"fsdp": d}, device_id_type=MESH)
    pl.semaphore_signal(sem, inc=1, device_id={"seq": 1 - c.s}, device_id_type=MESH)
    return len(devices) + 1


class Wires:
    def __init__(self, c, send_sem, recv_sem):
        self.c, self.send_sem, self.recv_sem = c, send_sem, recv_sem
        self.used, self.pending = 0, []

    def take(self, n):
        self.used += n
        return self.used - n

    def copy(self, src, dst, i, to):
        return pltpu.make_async_remote_copy(
            src_ref=src,
            dst_ref=dst,
            send_sem=self.send_sem.at[i],
            recv_sem=self.recv_sem.at[i],
            device_id=to,
            device_id_type=MESH,
        )

    def send(self, src, dst, i, to):
        to = to if isinstance(to, dict) else {"fsdp": to}
        d = self.copy(src, dst, i, to)
        d.start()
        self.pending.append(d)

    def wait(self, dst, i):
        self.copy(dst, dst, i, {"fsdp": self.c.f}).wait_recv()

    def finish(self):
        for d in self.pending:
            d.wait_send()


def gather_ring(w, block, halves, right, left, far, me, direct):
    i0 = w.take(4)
    bl, br, bo = (me + 3) % 4, (me + 1) % 4, (me + 2) % 4

    def send_all():
        for i, to in enumerate((right, left, far)):
            w.send(block(me), block(me), i0 + i, to)

    def wait_all():
        for i, k in enumerate((bl, br, bo)):
            w.wait(block(k), i0 + i)

    if direct:
        return [send_all, wait_all]

    def first():
        w.send(block(me), block(me), i0, right)
        w.send(block(me), block(me), i0 + 1, left)

    def second():
        w.wait(block(bl), i0)
        a = halves(bl)[0]
        w.send(a, a, i0 + 2, right)
        w.wait(block(br), i0 + 1)
        b = halves(br)[1]
        w.send(b, b, i0 + 3, left)

    def third():
        a, b = halves(bo)
        w.wait(a, i0 + 2)
        w.wait(b, i0 + 3)

    return [first, second, third]


def gather_pairs(w, half):
    c = w.c
    i0 = w.take(6)
    me, other = c.zl, 1 - c.zl

    def move(k, h, i, to):
        w.send(half(k, h), half(k, h), i0 + i, to)

    def got(k, h, i):
        w.wait(half(k, h), i0 + i)

    def s0():
        move(c.zh, other, 0, c.zo)

    def s1():
        got(c.ke, me, 0)
        move(c.ke, me, 2, c.zi)
        move(c.zh, me, 1, c.zo)

    def s2():
        got(c.kf, other, 2)
        move(c.kf, other, 4, c.zo)

    def s3():
        got(c.ke, other, 1)
        move(c.ke, other, 3, c.zi)

    def s4():
        got(c.kp, me, 4)
        move(c.kp, me, 5, c.zi)

    def s5():
        got(c.kf, me, 3)
        got(c.kp, other, 5)

    return [s0, s1, s2, s3, s4, s5]


def gather_relay(w, block, direct):
    c = w.c
    i0 = w.take(3)

    def send_all():
        for i, to in enumerate((c.zo, c.z2, c.z3)):
            w.send(block(c.zh), block(c.zh), i0 + i, to)

    def wait_all():
        for i, k in enumerate((c.ke, c.kf, c.kp)):
            w.wait(block(k), i0 + i)

    if direct:
        return [send_all, wait_all]

    def s0():
        w.send(block(c.zh), block(c.zh), i0, c.zo)

    def s1():
        w.wait(block(c.ke), i0)
        w.send(block(c.ke), block(c.ke), i0 + 1, c.zi)

    def s2():
        w.wait(block(c.kf), i0 + 1)
        w.send(block(c.kf), block(c.kf), i0 + 2, c.zo)

    def s3():
        w.wait(block(c.kp), i0 + 2)

    return [s0, s1, s2, s3]


def chain(*parts):
    steps = list(parts[0])
    for part in parts[1:]:
        last, then = steps.pop(), part[0]

        def both(last=last, then=then):
            last()
            then()

        steps += [both, *part[1:]]
    return steps


def named(events, name, steps):
    for i, fn in enumerate(steps):
        events[f"{name}{i}"] = fn


def gather_events(c, w, r):
    W, events = r.W, {}

    def stage(st):
        base = w.take(7)
        slab, held = getattr(r, f"gs{st}"), getattr(r, f"gh{st}")

        def start():
            for d in range(1, 8):
                dm = (c.m + d) % 8
                w.send(slab.at[dm % 4], held.at[c.m], base + d - 1, c.f - c.m + dm)
            held[c.m] = slab[c.y]

        def align():
            for d in range(1, 8):
                w.wait(held.at[(c.m + 8 - d) % 8], base + d - 1)
            row = lax.broadcasted_iota(jnp.int32, (48, 64), 0)
            col = lax.broadcasted_iota(jnp.int32, (48, 64), 1)
            pick = ((row // 6 == col // 8) & (row % 6 == col % 8)).astype(BF)
            for i in range(GATHER.slab[st]):
                v = held[:, i].reshape(64, 128)
                W[GATHER.tile(st, i, c.y), c.x, c.zh] = dot(pick, v).astype(BF)

        events[f"g{st}s"], events[f"g{st}a"] = start, align
        dz, dx, dw = GATHER.direct_z[st], GATHER.direct_x[st], GATHER.direct_wide[st]
        xa, xb = GATHER.x(st)
        za, zb = GATHER.z(st)
        zm = (za + zb + 1) // 2
        x = chain(
            gather_relay(w, lambda k: W.at[xa:xb, c.x, k], dz),
            gather_ring(
                w,
                lambda i: W.at[xa:xb, i],
                lambda i: (W.at[xa:xb, i, 0:2], W.at[xa:xb, i, 2:4]),
                c.xr,
                c.xl,
                c.xo,
                c.x,
                dw,
            ),
        )
        z = chain(
            gather_ring(
                w,
                lambda i: W.at[za:zb, i, c.zh],
                lambda i: (W.at[za:zm, i, c.zh], W.at[zm:zb, i, c.zh]),
                c.xr,
                c.xl,
                c.xo,
                c.x,
                dx,
            ),
            gather_pairs(w, lambda k, h: W.at[za:zb, pl.ds(2 * h, 2), k]),
        )
        mine = GATHER.y(st, c.y)
        y = chain(
            gather_relay(w, lambda k: W.at[mine, c.x, k], True),
            gather_ring(
                w,
                lambda i: W.at[mine, i],
                lambda i: (W.at[mine, i, 0:2], W.at[mine, i, 2:4]),
                c.xr,
                c.xl,
                c.xo,
                c.x,
                True,
            ),
            gather_ring(
                w,
                lambda i: W.at[GATHER.y(st, i)],
                lambda i: (W.at[GATHER.y(st, i), 0:2], W.at[GATHER.y(st, i), 2:4]),
                c.yr,
                c.yl,
                c.yo,
                c.y,
                dw,
            ),
        )
        named(events, f"g{st}x", x)
        named(events, f"g{st}y", y)
        named(events, f"g{st}z", z)

    for st in GATHER.stages:
        stage(st)
    return events


def gather_buffers():
    out = {}
    for st in GATHER.stages:
        out[f"gs{st}"] = ((4, GATHER.slab[st], 8, 128), BF)
        out[f"gh{st}"] = ((8, GATHER.slab[st], 8, 128), BF)
    return out


def fill_slab(c, r):
    zero = jnp.zeros((2, 128), BF)

    def vectors():
        lane = lax.broadcasted_iota(jnp.int32, (6, 128), 1)
        row = lax.broadcasted_iota(jnp.int32, (6, 128), 0)
        values = jnp.broadcast_to(r.vec[...].astype(F32), (6, 128))
        total = jnp.zeros((6, 128), F32)
        for col, at in [(0, row), (1, row + 6), (2, row + 12)] + [(4 + k, 18 + 4 * row + k) for k in range(4)]:
            v = jnp.sum(jnp.where(lane == at, values, 0.0), axis=1, keepdims=True)
            total = jnp.where(lane == col, v, total)
        return total.astype(BF)

    def tile(n):
        if n == VEC:
            return vectors()
        if n < 10:
            part, i = (n - 1) // 3, (n - 1) % 3
            return r.qkv[:, pl.ds(pl.multiple_of(part * 768 + c.s * 384 + i * 128, 128), 128)]
        if n < 13:
            return r.out[:, pl.ds(pl.multiple_of(c.s * 384 + (n - 10) * 128, 128), 128)]
        ref, i = (r.up, n - 13) if n < 25 else (r.down, n - 25)
        return ref[:, pl.ds(pl.multiple_of(c.s * 1536 + i * 128, 128), 128)]

    for st in GATHER.stages:
        slab = getattr(r, f"gs{st}")
        for i in range(GATHER.slab[st]):
            for j in range(4):
                if i < GATHER.ny[st] or j == 0:
                    v = tile(GATHER.tile(st, i, j))
                slab[j, i, 0:6] = v
                slab[j, i, 6:8] = zero


def rows_loop(fn, size=64):
    def body(i, carry):
        fn(pl.ds(pl.multiple_of(i * size, size), size))
        return carry

    lax.fori_loop(0, 512 // size, body, 0)


def dot(a, b):
    return jnp.dot(a, b, preferred_element_type=F32)


def dot_nt(a, b):
    return lax.dot_general(a, b, (((1,), (1,)), ((), ())), preferred_element_type=F32)


def dot_tn(a, b):
    return lax.dot_general(a, b, (((0,), (0,)), ((), ())), preferred_element_type=F32)


def wide(W, tiles, rows=None):
    parts = []
    for t in tiles:
        v = W[t].reshape(768, 128)
        parts.append(v if rows is None else v[rows[0] : rows[1]])
    return parts[0] if len(parts) == 1 else jnp.concatenate(parts, axis=1)


def pairs_of(tiles):
    return [(i, tiles[i : i + 2]) for i in range(0, len(tiles), 2)]


def partner_lanes(v):
    lane = lax.broadcasted_iota(jnp.int32, v.shape, 1) % 64
    return jnp.where(lane < 32, pltpu.roll(v, 96, 1), pltpu.roll(v, 32, 1))


def mean_of(v):
    return jnp.sum(v, axis=1, keepdims=True) * (1.0 / 768.0)


BLOCKS = ((0, 128, 0), (128, 256, 128), (256, 128, None), (384, 256, None))


class Held:
    pass


def layer_steps(c, w, r):
    s = c.s
    other = {"seq": 1 - s}
    own = pl.ds(pl.multiple_of(s * 256, 256), 256)
    oth = pl.ds(pl.multiple_of(256 - s * 256, 256), 256)
    i0 = w.take(6)
    W, G = r.W, r.G
    r.gm, r.gmb, r.ln2 = r.x, r.hid, r.dgiven
    r.dq, r.dk, r.dv = r.dgelu.at[0:2], r.dgelu.at[2:4], r.dgelu.at[4:6]
    steps = {}

    def step(fn):
        name = fn.__name__
        steps[f"{name}{sum(k.rstrip('0123456789') == name for k in steps)}"] = fn

    @step
    def exchange_rows():
        w.send(r.hidden, r.hid.at[own], i0, other)
        w.send(r.d_out, r.dgiven.at[own], i0 + 1, other)
        r.hid[own] = r.hidden[...]
        r.dgiven[own] = r.d_out[...]

    @step
    def tables():
        src = r.source[...]
        r.perm[...] = (lax.broadcasted_iota(jnp.int32, (512, 512), 0) == src).astype(BF)
        first_len = r.lengths[0, 0] * 16
        token = lax.broadcasted_iota(jnp.int32, (256, 256), 0)
        offset = jnp.where(token >= first_len, token - first_len, token)
        at_pos = (lax.broadcasted_iota(jnp.int32, (256, 256), 1) == offset).astype(BF)
        parts = dot(at_pos, r.table[...])
        cos_v = parts[:, 0:128] + parts[:, 128:256] + parts[:, 256:384]
        sin_v = parts[:, 384:512] + parts[:, 512:640] + parts[:, 640:768]
        r.cs[0:256], r.cs[256:512] = cos_v, cos_v
        r.sn[0:256], r.sn[256:512] = sin_v, sin_v
        row = lax.broadcasted_iota(jnp.int32, (512, 128), 0)
        lane = lax.broadcasted_iota(jnp.int32, (512, 128), 1)
        noisy = row < 256
        block = (row % 256) // 16
        first_blocks = r.lengths[0, 0]
        for h in range(2):
            col = lane - 64 * (1 - h)
            at = col % 16
            same = (block >= first_blocks) == (at >= first_blocks)
            clean_ok = same & ((at < block) | ((at == block) & ~noisy))
            ok = jnp.where(col < 16, clean_ok.astype(jnp.int32), (at == block).astype(jnp.int32))
            used = (col >= 0) & (col < 32)
            r.fq[h] = jnp.where(used & (ok == 0), NEG, 0.0).astype(BF)
            mine = jnp.where(noisy, block + 16, block)
            r.fk[h] = (used & (col == mine)).astype(BF)
        zero = jnp.zeros((128, 128), BF)
        for q in (0, 256):
            r.ds_c[0, q : q + 128, 128:256] = zero
            r.ds_c[1, q : q + 128, 128:256] = zero
            for head in range(6):
                r.ec[head, q : q + 128, 128:256] = zero

    @step
    def slot_order():
        w.wait(r.hid.at[oth], i0)
        for n in range(0, 768, 256):
            r.x[:, n : n + 256] = dot_tn(r.perm[...], r.hid[:, n : n + 256])

    @step
    def slot_order_grad():
        w.wait(r.dgiven.at[oth], i0 + 1)
        for n in range(0, 768, 256):
            r.dsl[:, n : n + 256] = dot_tn(r.perm[...], r.dgiven[:, n : n + 256]).astype(BF)
        r.dslT[...] = r.dsl[...].T
        r.grow[...] = jnp.sum(r.dsl[...].astype(F32), axis=0, keepdims=True)

    def norm(src_ref, n_ref, inv_ref, ln_ref, gain):
        def chunk(q):
            v = src_ref[q]
            cen = v - mean_of(v)
            inv = lax.rsqrt(mean_of(cen * cen) + EPS)
            nv = cen * inv
            n_ref[q] = nv
            inv_ref[q] = jnp.broadcast_to(inv, (64, 128))
            if ln_ref is not None:
                ln_ref[q] = (nv * r.vrow[gain : gain + 1]).astype(BF)

        rows_loop(chunk)

    @step
    def first_norm():
        norm(r.x, r.n1, r.inv1, None, 0)

    def ub_mask():
        d_of = lax.broadcasted_iota(jnp.int32, (384, 1536), 0)
        n_of = lax.broadcasted_iota(jnp.int32, (384, 1536), 1)
        spread = (
            lax.broadcasted_iota(jnp.int32, (128, 1536), 0)
            == 4 + lax.broadcasted_iota(jnp.int32, (128, 1536), 1) % 4
        ).astype(BF)
        return n_of // 4 == d_of, spread

    @step
    def vectors():
        r.vrow[...] = W[VEC].reshape(768, 128).astype(F32).T[0:8]

        def chunk(q):
            r.ln1[q] = (r.n1[q] * r.vrow[0:1]).astype(BF)

        rows_loop(chunk)

    first_all = lax.broadcasted_iota(jnp.int32, (512, 128), 1) < 64

    def qkv_step(i, tiles):
        def qkv():
            y = dot(r.ln1[...], wide(W, tiles))
            for k in range(len(tiles)):
                t = i + k
                v = y[:, 128 * k : 128 * k + 128].astype(BF)
                cols = slice(128 * (t % 3), 128 * (t % 3) + 128)
                if t >= 6:
                    one = jnp.ones_like(v)
                    r.v2[0, :, cols] = jnp.where(first_all, v, one)
                    r.v2[1, :, cols] = jnp.where(first_all, one, v)
                    continue
                f = v.astype(F32)
                f = (f * r.cs[...] + partner_lanes(f) * r.sn[...]).astype(BF)
                if t < 3:
                    f = f * 0.125
                to, fill = (r.q2, r.fq) if t < 3 else (r.k2, r.fk)
                to[0, :, cols] = jnp.where(first_all, f, fill[0])
                to[1, :, cols] = jnp.where(first_all, fill[1], f)

        return qkv

    for i, tiles in pairs_of(QKV):
        step(qkv_step(i, tiles))

    @step
    def up_bias():
        mask, spread = ub_mask()
        half_rows = W[VEC, pl.ds(2 * s, 2)].reshape(384, 128)
        r.ubrow[...] = jnp.sum(jnp.where(mask, dot(half_rows, spread), 0.0), axis=0, keepdims=True)

    lane = lax.broadcasted_iota(jnp.int32, (128, 128), 1)
    first = lane < 64

    def attend_step(p, blocks):
        def attend():
            cols = slice(128 * p, 128 * p + 128)
            items = [(slice(q0, q0 + 128), nc, k0, h) for q0, nc, k0 in blocks for h in range(2)]
            scores, outs = [], []
            for rows, nc, k0, h in items:
                q = r.q2[h, rows, cols]
                sc = dot_nt(q, r.k2[h, 256 : 256 + nc, cols])
                if k0 is not None:
                    sc = jnp.concatenate([sc, dot_nt(q, r.k2[h, k0 : k0 + 128, cols])], axis=1)
                scores.append(sc)
            tops = [jnp.max(sc, axis=1, keepdims=True) for sc in scores]
            exps = [jnp.exp(sc - top).astype(BF) for sc, top in zip(scores, tops)]
            for (rows, nc, k0, h), e in zip(items, exps):
                r.ec[2 * p + h, rows, 0:nc] = e[:, 0:nc]
                o = dot(e[:, 0:nc], r.v2[h, 256 : 256 + nc, cols])
                if k0 is not None:
                    r.en[2 * p + h, rows] = e[:, nc : nc + 128]
                    o = o + dot(e[:, nc : nc + 128], r.v2[h, k0 : k0 + 128, cols])
                outs.append(o)
            for i in range(0, len(items), 2):
                rows, one, two = items[i][0], outs[i], outs[i + 1]
                rec = 1.0 / jnp.where(first, pltpu.roll(one, 64, 1), pltpu.roll(two, 64, 1))
                r.rec[rows, cols] = rec
                r.att[rows, cols] = (jnp.where(first, one, two) * rec).astype(BF)

        return attend

    for p in range(3):
        step(attend_step(p, BLOCKS[:2]))
        step(attend_step(p, BLOCKS[2:]))

    @step
    def out_product():
        for n in range(0, 768, 256):
            y = dot_nt(r.att[...], wide(W, OUT, (n, n + 256)))
            r.part[:, n : n + 256] = y
            r.sendb[0, :, n : n + 256] = y.astype(BF)
        w.send(r.sendb.at[0], r.recvb.at[0], i0 + 2, other)

    @step
    def second_norm():
        w.wait(r.recvb.at[0], i0 + 2)

        def add_mid(q):
            r.middle[q] = r.x[q] + r.part[q] + r.recvb[0, q].astype(F32)

        rows_loop(add_mid)
        norm(r.middle, r.n2, r.inv2, r.ln2, 1)

    def up_step(i, tiles):
        def up():
            cols = slice(128 * i, 128 * i + 256)
            pre = dot(r.ln2[...], wide(W, tiles)) + r.ubrow[:, cols]
            sq = pre * pre
            th = jnp.tanh(0.7978845608028654 * (pre + 0.044715 * pre * sq))
            r.act[:, cols] = (0.5 * pre * (1.0 + th)).astype(BF)
            slope = 0.5 * (1.0 + th) + 0.5 * pre * (1.0 - th * th) * (
                0.7978845608028654 * (1.0 + 0.134145 * sq)
            )
            r.dgelu[i], r.dgelu[i + 1] = slope[:, 0:128], slope[:, 128:256]

        return up

    for i, tiles in pairs_of(UP):
        step(up_step(i, tiles))

    def store(tiles, y):
        for k, t in enumerate(tiles):
            G[t] = y[:, 128 * k : 128 * k + 128].astype(BF).reshape(4, 4, 48, 128)

    def weight_steps(name, tiles, leftT, right):
        def make(i, group):
            def fn():
                store(group, dot(leftT[...], right[:, 128 * i : 128 * (i + len(group))]))

            fn.__name__ = name
            return fn

        for i, group in pairs_of(tiles):
            step(make(i, group))

    weight_steps("grad_down", GDOWN, r.dslT, r.act)

    def down_back_step(i, tiles):
        def down_back():
            cols = slice(128 * i, 128 * i + 256)
            slope = jnp.concatenate([r.dgelu[i], r.dgelu[i + 1]], axis=1)
            g = (dot(r.dsl[...], wide(W, tiles)) * slope).astype(BF)
            r.gpre[:, cols] = g
            r.gub[:, cols] = jnp.sum(g.astype(F32), axis=0, keepdims=True)

        return down_back

    for i, tiles in pairs_of(DOWN):
        step(down_back_step(i, tiles))

    @step
    def up_back():
        for n in range(0, 768, 256):
            y = dot_nt(r.gpre[...], wide(W, UP, (n, n + 256)))
            r.part[:, n : n + 256] = y
            r.sendb[1, :, n : n + 256] = y.astype(BF)
        w.send(r.sendb.at[1], r.recvb.at[1], i0 + 3, other)

    @step
    def grad_vectors():
        rows = jnp.concatenate(
            [jnp.zeros((2, 768), F32), r.grow[...], jnp.zeros((125, 768), F32)], axis=0
        )
        G[GVEC] = rows.T.astype(BF).reshape(4, 4, 48, 128)
        mask, spread = ub_mask()
        ub = dot_nt(jnp.where(mask, r.gub[...], 0.0).astype(BF), spread)
        old = G[GVEC, pl.ds(2 * s, 2)].reshape(384, 128)
        G[GVEC, pl.ds(2 * s, 2)] = (old.astype(F32) + ub).astype(BF).reshape(2, 4, 48, 128)

    @step
    def lnb_t():
        r.lnbT[...] = r.ln2[...].T

    weight_steps("grad_up", GUP, r.lnbT, r.gpre)

    @step
    def middle_back():
        w.wait(r.recvb.at[1], i0 + 3)

        def mid_back(q):
            gl = r.part[q] + r.recvb[1, q].astype(F32)
            nv = r.n2[q]
            u = gl * r.vrow[1:2]
            g = r.dsl[q].astype(F32) + r.inv2[q][:, 0:1] * (u - mean_of(u) - nv * mean_of(u * nv))
            r.gm[q] = g
            r.gmb[q] = g.astype(BF)

        rows_loop(mid_back)

    @step
    def out_back():
        for i, tiles in pairs_of(OUT):
            r.gatt[:, 128 * i : 128 * (i + len(tiles))] = dot(r.gmb[...], wide(W, tiles)).astype(BF)

    @step
    def grad_out_t():
        r.gmT[...] = r.gmb[...].T

    weight_steps("grad_out", GOUT, r.gmT, r.att)

    def attend_prep_step(p):
        def attend_prep():
            cols = slice(128 * p, 128 * p + 128)
            ga = r.gatt[:, cols].astype(F32) * r.rec[:, cols]
            gb = ga.astype(BF)
            r.ga[:, cols] = gb
            t = gb.astype(F32) * r.att[:, cols].astype(F32)
            hi = t.astype(BF)
            lo = (t - hi.astype(F32)).astype(BF)
            li = lax.broadcasted_iota(jnp.int32, (128, 128), 0)
            lj = lax.broadcasted_iota(jnp.int32, (128, 128), 1)
            across = ((li < 64) != (lj < 64)).astype(BF)
            delta = -(dot(hi, across) + dot(lo, across))
            dh = delta.astype(BF)
            dl = (delta - dh.astype(F32)).astype(BF)
            ln = lax.broadcasted_iota(jnp.int32, (512, 128), 1) % 64
            fill = jnp.where(ln == 0, dh, jnp.where(ln == 1, dl, jnp.zeros_like(dh)))
            r.g2[0, :, cols] = jnp.where(first_all, gb, fill)
            r.g2[1, :, cols] = jnp.where(first_all, fill, gb)

        return attend_prep

    def attend_back_step(p, h):
        def attend_back():
            head = 2 * p + h
            cols = slice(128 * p, 128 * p + 128)
            items = [(slice(q0, q0 + 128), nc, k0) for q0, nc, k0 in BLOCKS]
            dps = []
            for rows, nc, k0 in items:
                g = r.g2[h, rows, cols]
                dp = dot_nt(g, r.v2[h, 256 : 256 + nc, cols])
                if k0 is not None:
                    dp = jnp.concatenate([dp, dot_nt(g, r.v2[h, k0 : k0 + 128, cols])], axis=1)
                dps.append(dp)
            ds = []
            for (rows, nc, k0), dp in zip(items, dps):
                e = r.ec[head, rows, 0:nc]
                if k0 is not None:
                    e = jnp.concatenate([e, r.en[head, rows]], axis=1)
                ds.append((e.astype(F32) * dp).astype(BF))
            for (rows, nc, k0), d in zip(items, ds):
                r.ds_c[h, rows, 0:nc] = d[:, 0:nc]
                o = dot(d[:, 0:nc], r.k2[h, 256 : 256 + nc, cols])
                if k0 is not None:
                    o = o + dot(d[:, nc : nc + 128], r.k2[h, k0 : k0 + 128, cols])
                    r.dk[h, rows] = dot_tn(d[:, nc : nc + 128], r.q2[h, rows, cols])
                    r.dv[h, rows] = dot_tn(r.en[head, rows], r.ga[rows, cols])
                r.dq[h, rows] = o
            r.dk[h, 256:512] = dot_tn(r.ds_c[h], r.q2[h, :, cols])
            r.dv[h, 256:512] = dot_tn(r.ec[head], r.ga[:, cols])

        return attend_back

    def attend_join_step(p):
        def attend_join():
            for i, (ref, scale) in enumerate(((r.dq, 0.125), (r.dk, 1.0))):
                v = jnp.where(first_all, ref[0], ref[1]) * scale
                v = v * r.cs[...] - partner_lanes(v) * r.sn[...]
                r.grows[:, 384 * i + 128 * p : 384 * i + 128 * p + 128] = v.astype(BF)
            v = jnp.where(first_all, r.dv[0], r.dv[1])
            r.grows[:, 768 + 128 * p : 768 + 128 * p + 128] = v.astype(BF)

        return attend_join

    for p in range(3):
        step(attend_prep_step(p))
        step(attend_back_step(p, 0))
        step(attend_back_step(p, 1))
        step(attend_join_step(p))

    @step
    def lna_t():
        r.lnaT[...] = r.ln1[...].T

    weight_steps("grad_qkv", GQKV, r.lnaT, r.grows)

    @step
    def qkv_back():
        for n in range(0, 768, 256):
            r.part[:, n : n + 256] = dot_nt(r.grows[...], wide(W, QKV, (n, n + 256)))

    @step
    def first_back():
        def chunk(q):
            gl = r.part[q]
            nv = r.n1[q]
            u = gl * r.vrow[0:1]
            r.part[q] = r.inv1[q][:, 0:1] * (u - mean_of(u) - nv * mean_of(u * nv))

        rows_loop(chunk)

    @step
    def hidden_other():
        r.half_out[0] = dot(r.perm[oth], r.part[...].astype(BF)).astype(BF)
        w.send(r.half_out.at[0], r.half_in.at[0], i0 + 4, other)

    def back_to_given(v):
        hi = v.astype(BF)
        lo = (v - hi.astype(F32)).astype(BF)
        return dot(r.perm[own], hi) + dot(r.perm[own], lo)

    @step
    def hidden_own():
        for n in range(0, 768, 256):
            r.grad_hidden[:, n : n + 256] = back_to_given(r.gm[:, n : n + 256] + r.part[:, n : n + 256])

    def down_product_step(n):
        def down_product():
            cols = slice(n, n + 256)
            y = dot_nt(r.act[...], wide(W, DOWN, (n, n + 256)))
            r.half_out[1, :, cols] = dot(r.perm[oth], y.astype(BF)).astype(BF)
            r.outp[:, cols] = back_to_given(y + r.middle[:, cols] + r.vrow[2:3, cols])
            if n == 512:
                w.send(r.half_out.at[1], r.half_in.at[1], i0 + 5, other)

        return down_product

    for n in (0, 256, 512):
        step(down_product_step(n))

    @step
    def outputs():
        w.wait(r.half_in.at[0], i0 + 4)
        r.grad_hidden[...] += r.half_in[0].astype(F32)
        w.wait(r.half_in.at[1], i0 + 5)
        r.output[...] = (r.outp[...] + r.half_in[1].astype(F32)).astype(BF)

    return steps


LAYER_BUFFERS = dict(
    hid=((512, 768), BF),
    dgiven=((512, 768), BF),
    perm=((512, 512), BF),
    x=((512, 768), F32),
    n1=((512, 768), F32),
    inv1=((512, 128), F32),
    ln1=((512, 768), BF),
    lnaT=((768, 512), BF),
    lnbT=((768, 512), BF),
    gmT=((768, 512), BF),
    dslT=((768, 512), BF),
    cs=((512, 128), F32),
    sn=((512, 128), F32),
    fq=((2, 512, 128), BF),
    fk=((2, 512, 128), BF),
    q2=((2, 512, 384), BF),
    k2=((2, 512, 384), BF),
    v2=((2, 512, 384), BF),
    ec=((6, 512, 256), BF),
    en=((6, 256, 128), BF),
    ds_c=((2, 512, 256), BF),
    rec=((512, 384), F32),
    ga=((512, 384), BF),
    g2=((2, 512, 384), BF),
    att=((512, 384), BF),
    part=((512, 768), F32),
    sendb=((2, 512, 768), BF),
    recvb=((2, 512, 768), BF),
    middle=((512, 768), F32),
    n2=((512, 768), F32),
    inv2=((512, 128), F32),
    act=((512, 1536), BF),
    dgelu=((12, 512, 128), F32),
    dsl=((512, 768), BF),
    gpre=((512, 1536), BF),
    gatt=((512, 384), BF),
    grows=((512, 1152), BF),
    outp=((256, 768), F32),
    half_in=((2, 256, 768), BF),
    half_out=((2, 256, 768), BF),
    vrow=((8, 768), F32),
    grow=((1, 768), F32),
    ubrow=((1, 1536), F32),
    gub=((1, 1536), F32),
)


def add_to(dst, *terms):
    total = dst[...].astype(F32)
    for t in terms:
        total = total + t[...].astype(F32)
    dst[...] = total.astype(BF)


def reduce_ring(w, block, halves, got, far, right, left, over, me, whole, direct):
    i0 = w.take(6)
    bl, br, bo = (me + 3) % 4, (me + 1) % 4, (me + 2) % 4

    def send_all():
        for i, (k, to) in enumerate(((br, right), (bl, left), (bo, over))):
            w.send(block(k), whole[i], i0 + i, to)

    def wait_all():
        for i in range(3):
            w.wait(whole[i], i0 + i)
        add_to(block(me), *whole)

    if direct:
        return [send_all, wait_all]
    (la, lb), (ra, rb) = got
    fl, fr = far

    def first():
        a, b = halves(bo)
        w.send(a, fl, i0, right)
        w.send(b, fr, i0 + 1, left)
        w.send(halves(br)[1], lb, i0 + 2, right)
        w.send(halves(bl)[0], ra, i0 + 3, left)

    def second():
        w.wait(fl, i0)
        a = halves(br)[0]
        add_to(a, fl)
        w.send(a, la, i0 + 4, right)
        w.wait(fr, i0 + 1)
        b = halves(bl)[1]
        add_to(b, fr)
        w.send(b, rb, i0 + 5, left)

    def third():
        a, b = halves(me)
        w.wait(lb, i0 + 2)
        w.wait(rb, i0 + 5)
        add_to(b, lb, rb)
        w.wait(ra, i0 + 3)
        w.wait(la, i0 + 4)
        add_to(a, la, ra)

    return [first, second, third]


def reduce_pairs(w, half, narrow, wide):
    c = w.c
    i0 = w.take(6)
    me, other = c.zl, 1 - c.zl

    def move(k, h, to, i, chip_id):
        w.send(half(k, h), to, i0 + i, chip_id)

    def got(k, h, ref, i):
        w.wait(ref, i0 + i)
        add_to(half(k, h), ref)

    def s0():
        move(c.kp, other, narrow(0), 0, c.zi)

    def s1():
        got(c.kp, me, narrow(0), 0)
        move(c.kp, me, narrow(1), 2, c.zo)
        move(c.kf, me, wide(0, me), 1, c.zi)

    def s2():
        got(c.kf, other, narrow(1), 2)
        move(c.kf, other, wide(0, other), 4, c.zi)

    def s3():
        got(c.ke, other, wide(0, other), 1)
        move(c.ke, other, wide(1, other), 3, c.zo)

    def s4():
        got(c.ke, me, wide(0, me), 4)
        move(c.ke, me, wide(1, me), 5, c.zo)

    def s5():
        got(c.zh, me, wide(1, me), 3)
        got(c.zh, other, wide(1, other), 5)

    return [s0, s1, s2, s3, s4, s5]


def reduce_relay(w, block, got, direct):
    c = w.c
    i0 = w.take(3)

    def send_all():
        for i, (k, to) in enumerate(((c.ke, c.zo), (c.kf, c.z2i), (c.kp, c.z3))):
            w.send(block(k), got[i], i0 + i, to)

    def wait_all():
        for i in range(3):
            w.wait(got[i], i0 + i)
        add_to(block(c.zh), *got)

    if direct:
        return [send_all, wait_all]

    def s0():
        w.send(block(c.kp), got[0], i0, c.zo)

    def s1():
        w.wait(got[0], i0)
        add_to(block(c.kf), got[0])
        w.send(block(c.kf), got[1], i0 + 1, c.zi)

    def s2():
        w.wait(got[1], i0 + 1)
        add_to(block(c.ke), got[1])
        w.send(block(c.ke), got[2], i0 + 2, c.zo)

    def s3():
        w.wait(got[2], i0 + 2)
        add_to(block(c.zh), got[2])

    return [s0, s1, s2, s3]


def reduce_events(c, w, r):
    G, events = r.G, {}

    def stage(st):
        dz, dx, dw = REDUCE.direct_z[st], REDUCE.direct_x[st], REDUCE.direct_wide[st]
        xa, xb = REDUCE.x(st)
        za, zb = REDUCE.z(st)
        nz = zb - za
        zm = (nz + 1) // 2

        def buf(name):
            return getattr(r, f"r{st}{name}")

        def sides(ref, cut):
            return [(ref.at[(i, slice(None), slice(0, cut))], ref.at[(i, slice(None), slice(cut, 2 * cut))]) for i in range(2)]

        bx, bxf, bxz = buf("x"), buf("xf"), buf("xz")
        x = chain(
            reduce_ring(
                w,
                lambda i: G.at[xa:xb, i],
                lambda i: (G.at[xa:xb, i, 0:2], G.at[xa:xb, i, 2:4]),
                sides(bx, 2),
                (bxf.at[0], bxf.at[1]),
                c.xr,
                c.xl,
                c.xo,
                c.x,
                [bx.at[i] for i in range(3)] if dw else None,
                dw,
            ),
            reduce_relay(w, lambda k: G.at[xa:xb, c.x, k], [bxz.at[i] for i in range(3)], dz),
        )
        bz, bzh, bzx = buf("z"), buf("zh"), buf("zx")
        z = chain(
            reduce_pairs(
                w,
                lambda k, h: G.at[za:zb, pl.ds(2 * h, 2), k],
                lambda i: bzh.at[i],
                lambda i, h: bz.at[i, :, pl.ds(2 * h, 2)],
            ),
            reduce_ring(
                w,
                lambda i: G.at[za:zb, i, c.zh],
                lambda i: (G.at[za : za + zm, i, c.zh], G.at[za + zm : zb, i, c.zh]),
                [(bzx.at[i, 0:zm], bzx.at[i, zm:nz]) for i in range(2)],
                (bzx.at[2, 0:zm], bzx.at[2, zm:nz]),
                c.xr,
                c.xl,
                c.xo,
                c.x,
                [bzx.at[i] for i in range(3)] if dx else None,
                dx,
            ),
        )
        mine = REDUCE.y(st, c.y)
        by, byf, byx, byxf, byz = buf("y"), buf("yf"), buf("yx"), buf("yxf"), buf("yz")
        y = chain(
            reduce_ring(
                w,
                lambda i: G.at[REDUCE.y(st, i)],
                lambda i: (G.at[REDUCE.y(st, i), 0:2], G.at[REDUCE.y(st, i), 2:4]),
                sides(by, 2),
                (byf.at[0], byf.at[1]),
                c.yr,
                c.yl,
                c.yo,
                c.y,
                [by.at[i] for i in range(3)] if dw else None,
                dw,
            ),
            reduce_ring(
                w,
                lambda i: G.at[mine, i],
                lambda i: (G.at[mine, i, 0:2], G.at[mine, i, 2:4]),
                sides(byx, 2),
                (byxf.at[0], byxf.at[1]),
                c.xr,
                c.xl,
                c.xo,
                c.x,
                [byx.at[i] for i in range(3)],
                True,
            ),
            reduce_relay(w, lambda k: G.at[mine, c.x, k], [byz.at[i] for i in range(3)], True),
        )

        def group(name, a, b):
            base = w.take(7)
            slab, held = buf("s" + name), buf("h" + name)

            def spread():
                row = lax.broadcasted_iota(jnp.int32, (64, 48), 0)
                col = lax.broadcasted_iota(jnp.int32, (64, 48), 1)
                pick = ((col // 6 == row // 8) & (col % 6 == row % 8)).astype(BF)
                for i in range(a, b):
                    o = dot(pick, G[REDUCE.tile(st, i, c.y), c.x, c.zh]).astype(BF)
                    slab[:, i - a] = o.reshape(8, 8, 128)
                for d in range(1, 8):
                    dm = (c.m + d) % 8
                    w.send(slab.at[dm], held.at[c.m], base + d - 1, c.f - c.m + dm)
                held[c.m] = slab[c.m]

            def collect():
                for d in range(1, 8):
                    w.wait(held.at[(c.m + 8 - d) % 8], base + d - 1)
                for i in range(a, b):
                    v = held[:, i - a].astype(F32)
                    if i < REDUCE.ny[st]:
                        for j in range(4):
                            r.done[c.s, REDUCE.tile(st, i, j)] = v[j] + v[j + 4]
                    else:
                        r.done[c.s, REDUCE.tile(st, i, 0)] = jnp.sum(v, axis=0)

            return [spread, collect]

        ny, nx = REDUCE.ny[st], REDUCE.nx[st]
        named(events, f"r{st}y", chain(y, group("y", 0, ny)))
        named(events, f"r{st}x", chain(x, group("x", ny, ny + nx)))
        named(events, f"r{st}z", chain(z, group("z", ny + nx, ny + nx + nz)))
        i0 = w.take(1)
        tiles = slice(REDUCE.first[st], REDUCE.first[st] + 4 * ny + nx + nz)

        def share():
            w.send(r.done.at[c.s, tiles], r.done.at[c.s, tiles], i0, {"seq": 1 - c.s})

        def shared():
            w.wait(r.done.at[1 - c.s, tiles], i0)

        named(events, f"r{st}d", [share, shared])

    for st in REDUCE.stages:
        stage(st)
    return events


def reduce_buffers():
    out = {}
    for st in REDUCE.stages:
        ny, nx, nz = REDUCE.ny[st], REDUCE.nx[st], REDUCE.nz[st]
        for name, dims in dict(
            x=(2 + REDUCE.direct_wide[st], nx, 4, 48, 128),
            xf=(2, nx, 2, 48, 128),
            xz=(3, nx, 48, 128),
            z=(2, nz, 4, 48, 128),
            zh=(2, nz, 2, 48, 128),
            zx=(3, nz, 48, 128),
            y=(2 + REDUCE.direct_wide[st], ny, 4, 4, 48, 128),
            yf=(2, ny, 2, 4, 48, 128),
            yx=(3, ny, 4, 48, 128),
            yxf=(2, ny, 2, 48, 128),
            yz=(3, ny, 48, 128),
            sx=(8, nx, 8, 128),
            hx=(8, nx, 8, 128),
            sy=(8, ny, 8, 128),
            hy=(8, ny, 8, 128),
            sz=(8, nz, 8, 128),
            hz=(8, nz, 8, 128),
        ).items():
            out[f"r{st}{name}"] = (dims, BF)
    return out


def rotary_table():
    freq = np.power(np.float32(10000.0), -2.0 * np.arange(32, dtype=np.float32) / np.float32(64))
    angle = np.arange(256, dtype=np.float32)[:, None] * freq.astype(np.float32)[None, :]
    cos, sin = np.cos(angle).astype(np.float32), np.sin(angle).astype(np.float32)
    terms = []
    for v in (np.concatenate([cos] * 4, axis=1), np.concatenate([-sin, sin] * 2, axis=1)):
        for _ in range(3):
            low = v.astype(BF)
            terms.append(low)
            v = v - low.astype(np.float32)
    return np.concatenate(terms, axis=1)


SCHEDULE = (
    77, 0, 1, 2, 97, 78, 3, 85, 90, 79, 98, 91, 80, 86, 105, 110, 99, 81, 106, 82, 87, 92, 111, 100, 88, 93, 94, 107,
    101, 112, 89, 83, 95, 102, 84, 113, 96, 4, 5, 114, 108, 6, 7, 8, 9, 10, 11, 12, 13, 14, 15, 16, 17, 109, 63, 103,
    115, 18, 104, 39, 116, 19, 20, 21, 22, 23, 24, 25, 26, 27, 28, 29, 30, 31, 32, 33, 34, 35, 36, 37, 38, 40, 41,
    42, 43, 44, 45, 123, 117, 130, 73, 46, 47, 48, 49, 50, 51, 52, 53, 54, 55, 56, 131, 57, 58, 59, 60, 61, 62, 64,
    65, 66, 118, 67, 68, 140, 153, 146, 124, 132, 133, 69, 70, 71, 72, 74, 154, 75, 141, 134, 147, 119, 125, 155,
    156, 76, 142, 157, 148, 126, 120, 135, 143, 149, 127, 144, 150, 158, 121, 136, 128, 122, 151, 137, 145, 159, 152,
    129, 138, 160, 161, 139, 162,
)

INPUTS = ("hidden", "d_out", "lengths", "source", "table", "qkv", "out", "up", "down", "vec")
OUTPUTS = ("output", "grad_hidden", "done")
BUFFERS = {
    "W": ((NT, 4, 4, 48, 128), BF),
    "G": ((NT, 4, 4, 48, 128), BF),
    **LAYER_BUFFERS,
    **gather_buffers(),
    **reduce_buffers(),
}
SEMS = 6 + 35 * len(GATHER.stages) + 58 * len(REDUCE.stages)


def step_kernel(*refs):
    r = Held()
    for name, ref in zip(INPUTS + OUTPUTS + tuple(BUFFERS), refs):
        setattr(r, name, ref)
    c = place()
    w = Wires(c, refs[-2], refs[-1])
    greeted = greet(c)
    events = {**layer_steps(c, w, r), **gather_events(c, w, r), **reduce_events(c, w, r)}
    fill_slab(c, r)
    events.pop("tables0")()
    pl.semaphore_wait(pltpu.get_barrier_semaphore(), greeted)
    steps = list(events.values())
    assert sorted(SCHEDULE) == list(range(len(steps)))
    for i in SCHEDULE:
        steps[i]()
    w.finish()


def finish_kernel(
    out_in, hidden_in, done, qkv, up, vec, out, hidden, gqkv, gout, gup, gdown, g1, g2, gub, gdb
):
    out[...] = out_in[...]
    hidden[...] = hidden_in[...]
    for core in range(2):
        for i, t in enumerate(GQKV):
            n = (i // 3) * 768 + core * 384 + (i % 3) * 128
            gqkv[:, n : n + 128] = done[core, t, 0:6]
        for tiles, ref, half in ((GOUT, gout, 384), (GUP, gup, 1536), (GDOWN, gdown, 1536)):
            for i, t in enumerate(tiles):
                n = core * half + i * 128
                ref[:, n : n + 128] = done[core, t, 0:6]
    lane = lax.broadcasted_iota(jnp.int32, (6, 128), 1)
    row = lax.broadcasted_iota(jnp.int32, (6, 128), 0)
    one = done[0, GVEC, 0:6]
    both = one + done[1, GVEC, 0:6]
    values = jnp.broadcast_to(vec[...].astype(F32), (6, 128))

    def as_row(places):
        total = jnp.zeros((6, 128), F32)
        for v, at in places:
            total = jnp.where(lane == at, v, total)
        return jnp.sum(total, axis=0)

    def gain_grad(weight, grad, first):
        gain = jnp.sum(jnp.where(lane == row + first, values, 0.0), axis=1, keepdims=True)
        return jnp.sum(weight[...].astype(F32) * grad[...], axis=1, keepdims=True) / gain

    g1[...] = as_row([(gain_grad(qkv, gqkv, 0), row)])[0:6]
    g2[...] = as_row([(gain_grad(up, gup, 6), row)])[0:6]
    gdb[...] = as_row([(one[:, 2:3], row)])[0:6]
    gub[...] = as_row([(both[:, 4 + k : 5 + k], 4 * row + k) for k in range(4)])[0:24]


VM = pl.BlockSpec(memory_space=pltpu.VMEM)
LIMIT = 62 * 2**20


def shape(dims, dtype=F32):
    return jax.ShapeDtypeStruct(dims, dtype)


def per_device(
    hidden, d_out, lengths, slot_source, first_gain, qkv_weight, out_weight, second_gain, up_weight, up_bias,
    down_weight, down_bias,
):
    vec = jnp.concatenate([first_gain, second_gain, down_bias, up_bias, jnp.zeros((86,), BF)])[None]
    parts = pl.pallas_call(
        step_kernel,
        out_shape=(shape((256, 768), BF), shape((256, 768)), shape((2, NT, 8, 128))),
        in_specs=[VM, VM, pl.BlockSpec(memory_space=pltpu.SMEM)] + [VM] * 7,
        out_specs=(VM,) * 3,
        scratch_shapes=[pltpu.VMEM(*v) for v in BUFFERS.values()] + [pltpu.SemaphoreType.DMA((SEMS,))] * 2,
        compiler_params=pltpu.CompilerParams(collective_id=0, has_side_effects=True, vmem_limit_bytes=LIMIT),
    )(
        hidden[0], d_out[0], lengths, slot_source, rotary_table(),
        qkv_weight, out_weight.T, up_weight, down_weight.T, vec,
    )
    output, grad_hidden, gqkv, gout, gup, gdown, g1, g2, gub, gdb = pl.pallas_call(
        finish_kernel,
        out_shape=(
            shape((256, 768), BF),
            shape((256, 768)),
            shape((6, 2304)),
            shape((6, 768)),
            shape((6, 3072)),
            shape((6, 3072)),
            shape((6,)),
            shape((6,)),
            shape((24,)),
            shape((6,)),
        ),
        in_specs=[VM] * 6,
        out_specs=(VM,) * 10,
    )(*parts, qkv_weight, up_weight, vec)
    return (output[None], grad_hidden[None], g1, gqkv, gout.T, g2, gup, gub, gdown.T, gdb)


def solution(mesh):
    return jax.shard_map(
        per_device,
        mesh=mesh,
        in_specs=(
            P("fsdp", "seq", None),
            P("fsdp", "seq", None),
            P("fsdp", None),
            P("fsdp", None),
            P("fsdp"),
            P("fsdp", None),
            P(None, "fsdp"),
            P("fsdp"),
            P("fsdp", None),
            P("fsdp"),
            P(None, "fsdp"),
            P("fsdp"),
        ),
        out_specs=(
            P("fsdp", "seq", None),
            P("fsdp", "seq", None),
            P("fsdp"),
            P("fsdp", None),
            P(None, "fsdp"),
            P("fsdp"),
            P("fsdp", None),
            P("fsdp"),
            P(None, "fsdp"),
            P("fsdp"),
        ),
        check_vma=False,
    )
```

```python
import jax
import jax.numpy as jnp
import numpy as np
from jax import lax
from jax.experimental import pallas as pl
from jax.experimental.pallas import tpu as pltpu
from jax.sharding import PartitionSpec as P

MESH = pl.DeviceIdType.MESH
BF = jnp.bfloat16
F32 = jnp.float32
EPS = 1e-05
NEG = -1e30

NT = 37
VEC, QKV, OUT, UP, DOWN = 0, list(range(1, 10)), [10, 11, 12], list(range(13, 25)), list(range(25, 37))
GVEC, GQKV, GOUT, GUP, GDOWN = 24, list(range(28, 37)), [25, 26, 27], list(range(12, 24)), list(range(12))


class Split:
    def __init__(self, ny, nx, nz, direct_z, direct_x, direct_wide):
        self.ny, self.nx, self.nz = ny, nx, nz
        self.direct_z, self.direct_x, self.direct_wide = direct_z, direct_x, direct_wide
        self.stages = range(len(ny))
        self.first = [sum(4 * ny[i] + nx[i] + nz[i] for i in range(st)) for st in self.stages]
        self.slab = [ny[i] + nx[i] + nz[i] for i in self.stages]

    def x(self, st):
        a = self.first[st] + 4 * self.ny[st]
        return a, a + self.nx[st]

    def z(self, st):
        a = self.first[st] + 4 * self.ny[st] + self.nx[st]
        return a, a + self.nz[st]

    def y(self, st, j):
        return pl.ds(self.first[st] + j * self.ny[st], self.ny[st])

    def tile(self, st, i, y):
        if i < self.ny[st]:
            return self.first[st] + y * self.ny[st] + i
        return self.first[st] + 3 * self.ny[st] + i


GATHER = Split((1, 2), (5, 9), (4, 7), (0, 0), (1, 1), (0, 0))
REDUCE = Split((2, 1), (9, 4), (8, 4), (0, 0), (1, 1), (0, 0))


class Place:
    pass


def chip(x, z, y):
    return x * 32 + z * 4 + y


def place():
    c = Place()
    c.f = lax.axis_index("fsdp")
    c.s = lax.axis_index("seq")
    c.x = c.f // 32
    c.z = (c.f // 4) % 8
    c.y = c.f % 4
    c.zh = c.z // 2
    c.zl = c.z % 2
    c.m = c.f % 8
    sgn = 2 * c.zl - 1
    c.xr = chip((c.x + 1) % 4, c.z, c.y)
    c.xl = chip((c.x + 3) % 4, c.z, c.y)
    c.xo = chip((c.x + 2) % 4, c.z, c.y)
    c.yo = chip(c.x, c.z, (c.y + 2) % 4)
    c.yr = chip(c.x, c.z, (c.y + 1) % 4)
    c.yl = chip(c.x, c.z, (c.y + 3) % 4)
    c.zo = chip(c.x, (c.z + 8 + sgn) % 8, c.y)
    c.zi = chip(c.x, (c.z + 8 - sgn) % 8, c.y)
    c.z2 = chip(c.x, (c.z + 8 + 2 * sgn) % 8, c.y)
    c.z2i = chip(c.x, (c.z + 8 - 2 * sgn) % 8, c.y)
    c.z3 = chip(c.x, (c.z + 8 + 3 * sgn) % 8, c.y)
    c.ke = (c.zh + 4 + sgn) % 4
    c.kf = (c.zh + 4 - sgn) % 4
    c.kp = (c.zh + 2) % 4
    return c


def greet(c):
    sem = pltpu.get_barrier_semaphore()
    group = [c.f - c.m + (c.m + d) % 8 for d in range(1, 8)]
    devices = [c.xr, c.xl, c.xo, c.zo, c.z2, c.z2i, c.z3] + group
    for d in devices:
        pl.semaphore_signal(sem, inc=1, device_id={"fsdp": d}, device_id_type=MESH)
    pl.semaphore_signal(sem, inc=1, device_id={"seq": 1 - c.s}, device_id_type=MESH)
    return len(devices) + 1


class Wires:
    def __init__(self, c, send_sem, recv_sem):
        self.c, self.send_sem, self.recv_sem = c, send_sem, recv_sem
        self.used, self.pending = 0, []

    def take(self, n):
        self.used += n
        return self.used - n

    def copy(self, src, dst, i, to):
        return pltpu.make_async_remote_copy(
            src_ref=src,
            dst_ref=dst,
            send_sem=self.send_sem.at[i],
            recv_sem=self.recv_sem.at[i],
            device_id=to,
            device_id_type=MESH,
        )

    def send(self, src, dst, i, to):
        to = to if isinstance(to, dict) else {"fsdp": to}
        d = self.copy(src, dst, i, to)
        d.start()
        self.pending.append(d)

    def wait(self, dst, i):
        self.copy(dst, dst, i, {"fsdp": self.c.f}).wait_recv()

    def finish(self):
        for d in self.pending:
            d.wait_send()


def gather_ring(w, block, halves, right, left, far, me, direct):
    i0 = w.take(4)
    bl, br, bo = (me + 3) % 4, (me + 1) % 4, (me + 2) % 4

    def send_all():
        for i, to in enumerate((right, left, far)):
            w.send(block(me), block(me), i0 + i, to)

    def wait_all():
        for i, k in enumerate((bl, br, bo)):
            w.wait(block(k), i0 + i)

    if direct:
        return [send_all, wait_all]

    def first():
        w.send(block(me), block(me), i0, right)
        w.send(block(me), block(me), i0 + 1, left)

    def second():
        w.wait(block(bl), i0)
        a = halves(bl)[0]
        w.send(a, a, i0 + 2, right)
        w.wait(block(br), i0 + 1)
        b = halves(br)[1]
        w.send(b, b, i0 + 3, left)

    def third():
        a, b = halves(bo)
        w.wait(a, i0 + 2)
        w.wait(b, i0 + 3)

    return [first, second, third]


def gather_pairs(w, half):
    c = w.c
    i0 = w.take(6)
    me, other = c.zl, 1 - c.zl

    def move(k, h, i, to):
        w.send(half(k, h), half(k, h), i0 + i, to)

    def got(k, h, i):
        w.wait(half(k, h), i0 + i)

    def s0():
        move(c.zh, other, 0, c.zo)

    def s1():
        got(c.ke, me, 0)
        move(c.ke, me, 2, c.zi)
        move(c.zh, me, 1, c.zo)

    def s2():
        got(c.kf, other, 2)
        move(c.kf, other, 4, c.zo)

    def s3():
        got(c.ke, other, 1)
        move(c.ke, other, 3, c.zi)

    def s4():
        got(c.kp, me, 4)
        move(c.kp, me, 5, c.zi)

    def s5():
        got(c.kf, me, 3)
        got(c.kp, other, 5)

    return [s0, s1, s2, s3, s4, s5]


def gather_relay(w, block, direct):
    c = w.c
    i0 = w.take(3)

    def send_all():
        for i, to in enumerate((c.zo, c.z2, c.z3)):
            w.send(block(c.zh), block(c.zh), i0 + i, to)

    def wait_all():
        for i, k in enumerate((c.ke, c.kf, c.kp)):
            w.wait(block(k), i0 + i)

    if direct:
        return [send_all, wait_all]

    def s0():
        w.send(block(c.zh), block(c.zh), i0, c.zo)

    def s1():
        w.wait(block(c.ke), i0)
        w.send(block(c.ke), block(c.ke), i0 + 1, c.zi)

    def s2():
        w.wait(block(c.kf), i0 + 1)
        w.send(block(c.kf), block(c.kf), i0 + 2, c.zo)

    def s3():
        w.wait(block(c.kp), i0 + 2)

    return [s0, s1, s2, s3]


def chain(*parts):
    steps = list(parts[0])
    for part in parts[1:]:
        last, then = steps.pop(), part[0]

        def both(last=last, then=then):
            last()
            then()

        steps += [both, *part[1:]]
    return steps


def named(events, name, steps):
    for i, fn in enumerate(steps):
        events[f"{name}{i}"] = fn


def gather_events(c, w, r):
    W, events = r.W, {}

    def stage(st):
        base = w.take(7)
        slab, held = getattr(r, f"gs{st}"), getattr(r, f"gh{st}")

        def start():
            for d in range(1, 8):
                dm = (c.m + d) % 8
                w.send(slab.at[dm % 4], held.at[c.m], base + d - 1, c.f - c.m + dm)
            held[c.m] = slab[c.y]

        def align():
            for d in range(1, 8):
                w.wait(held.at[(c.m + 8 - d) % 8], base + d - 1)
            row = lax.broadcasted_iota(jnp.int32, (48, 64), 0)
            col = lax.broadcasted_iota(jnp.int32, (48, 64), 1)
            pick = ((row // 6 == col // 8) & (row % 6 == col % 8)).astype(BF)
            for i in range(GATHER.slab[st]):
                v = held[:, i].reshape(64, 128)
                W[GATHER.tile(st, i, c.y), c.x, c.zh] = dot(pick, v).astype(BF)

        events[f"g{st}s"], events[f"g{st}a"] = start, align
        dz, dx, dw = GATHER.direct_z[st], GATHER.direct_x[st], GATHER.direct_wide[st]
        xa, xb = GATHER.x(st)
        za, zb = GATHER.z(st)
        zm = (za + zb + 1) // 2
        x = chain(
            gather_relay(w, lambda k: W.at[xa:xb, c.x, k], dz),
            gather_ring(
                w,
                lambda i: W.at[xa:xb, i],
                lambda i: (W.at[xa:xb, i, 0:2], W.at[xa:xb, i, 2:4]),
                c.xr,
                c.xl,
                c.xo,
                c.x,
                dw,
            ),
        )
        z = chain(
            gather_ring(
                w,
                lambda i: W.at[za:zb, i, c.zh],
                lambda i: (W.at[za:zm, i, c.zh], W.at[zm:zb, i, c.zh]),
                c.xr,
                c.xl,
                c.xo,
                c.x,
                dx,
            ),
            gather_pairs(w, lambda k, h: W.at[za:zb, pl.ds(2 * h, 2), k]),
        )
        mine = GATHER.y(st, c.y)
        y = chain(
            gather_relay(w, lambda k: W.at[mine, c.x, k], True),
            gather_ring(
                w,
                lambda i: W.at[mine, i],
                lambda i: (W.at[mine, i, 0:2], W.at[mine, i, 2:4]),
                c.xr,
                c.xl,
                c.xo,
                c.x,
                True,
            ),
            gather_ring(
                w,
                lambda i: W.at[GATHER.y(st, i)],
                lambda i: (W.at[GATHER.y(st, i), 0:2], W.at[GATHER.y(st, i), 2:4]),
                c.yr,
                c.yl,
                c.yo,
                c.y,
                dw,
            ),
        )
        named(events, f"g{st}x", x)
        named(events, f"g{st}y", y)
        named(events, f"g{st}z", z)

    for st in GATHER.stages:
        stage(st)
    return events


def gather_buffers():
    out = {}
    for st in GATHER.stages:
        out[f"gs{st}"] = ((4, GATHER.slab[st], 8, 128), BF)
        out[f"gh{st}"] = ((8, GATHER.slab[st], 8, 128), BF)
    return out


def column(ref, step, first):
    lane = lax.broadcasted_iota(jnp.int32, (6, 6 * step), 1)
    row = lax.broadcasted_iota(jnp.int32, (6, 6 * step), 0)
    values = jnp.broadcast_to(ref[...].astype(F32), (6, 6 * step))
    return jnp.sum(jnp.where(lane == step * row + first, values, 0.0), axis=1, keepdims=True)


def fill_slab(c, r):
    zero = jnp.zeros((2, 128), BF)

    def vectors():
        lane = lax.broadcasted_iota(jnp.int32, (6, 128), 1)
        total = jnp.zeros((6, 128), F32)
        for col, ref in ((0, r.gain_one), (1, r.gain_two), (2, r.down_bias)):
            total = jnp.where(lane == col, column(ref, 1, 0), total)
        for k in range(4):
            total = jnp.where(lane == 4 + k, column(r.up_bias, 4, k), total)
        return total.astype(BF)

    def tile(n):
        if n == VEC:
            return vectors()
        if n < 10:
            part, i = (n - 1) // 3, (n - 1) % 3
            return r.qkv[:, pl.ds(pl.multiple_of(part * 768 + c.s * 384 + i * 128, 128), 128)]
        if n < 13:
            return r.out[:, pl.ds(pl.multiple_of(c.s * 384 + (n - 10) * 128, 128), 128)]
        ref, i = (r.up, n - 13) if n < 25 else (r.down, n - 25)
        return ref[:, pl.ds(pl.multiple_of(c.s * 1536 + i * 128, 128), 128)]

    for st in GATHER.stages:
        slab = getattr(r, f"gs{st}")
        for i in range(GATHER.slab[st]):
            for j in range(4):
                if i < GATHER.ny[st] or j == 0:
                    v = tile(GATHER.tile(st, i, j))
                slab[j, i, 0:6] = v
                slab[j, i, 6:8] = zero


def rows_loop(fn, size=64):
    def body(i, carry):
        fn(pl.ds(pl.multiple_of(i * size, size), size))
        return carry

    lax.fori_loop(0, 512 // size, body, 0)


def dot(a, b):
    return jnp.dot(a, b, preferred_element_type=F32)


def dot_nt(a, b):
    return lax.dot_general(a, b, (((1,), (1,)), ((), ())), preferred_element_type=F32)


def dot_tn(a, b):
    return lax.dot_general(a, b, (((0,), (0,)), ((), ())), preferred_element_type=F32)


def wide(W, tiles, rows=None):
    parts = []
    for t in tiles:
        v = W[t].reshape(768, 128)
        parts.append(v if rows is None else v[rows[0] : rows[1]])
    return parts[0] if len(parts) == 1 else jnp.concatenate(parts, axis=1)


def pairs_of(tiles):
    return [(i, tiles[i : i + 2]) for i in range(0, len(tiles), 2)]


def partner_lanes(v):
    lane = lax.broadcasted_iota(jnp.int32, v.shape, 1) % 64
    return jnp.where(lane < 32, pltpu.roll(v, 96, 1), pltpu.roll(v, 32, 1))


def mean_of(v):
    return jnp.sum(v, axis=1, keepdims=True) * (1.0 / 768.0)


BLOCKS = ((0, 128, 0), (128, 256, 128), (256, 128, None), (384, 256, None))


class Held:
    pass


def layer_steps(c, w, r):
    s = c.s
    other = {"seq": 1 - s}
    own = pl.ds(pl.multiple_of(s * 256, 256), 256)
    oth = pl.ds(pl.multiple_of(256 - s * 256, 256), 256)
    i0 = w.take(6)
    W, G = r.W, r.G
    r.gm, r.gmb, r.ln2 = r.x, r.hid, r.dgiven
    r.dq, r.dk, r.dv = r.dgelu.at[0:2], r.dgelu.at[2:4], r.dgelu.at[4:6]
    steps = {}

    def step(fn):
        name = fn.__name__
        steps[f"{name}{sum(k.rstrip('0123456789') == name for k in steps)}"] = fn

    @step
    def exchange_rows():
        w.send(r.hidden, r.hid.at[own], i0, other)
        w.send(r.d_out, r.dgiven.at[own], i0 + 1, other)
        r.hid[own] = r.hidden[...]
        r.dgiven[own] = r.d_out[...]

    @step
    def tables():
        src = r.source[...]
        r.perm[...] = (lax.broadcasted_iota(jnp.int32, (512, 512), 0) == src).astype(BF)
        first_len = r.lengths[0, 0] * 16
        token = lax.broadcasted_iota(jnp.int32, (256, 256), 0)
        offset = jnp.where(token >= first_len, token - first_len, token)
        at_pos = (lax.broadcasted_iota(jnp.int32, (256, 256), 1) == offset).astype(BF)
        parts = dot(at_pos, r.table[...])
        cos_v = parts[:, 0:128] + parts[:, 128:256] + parts[:, 256:384]
        sin_v = parts[:, 384:512] + parts[:, 512:640] + parts[:, 640:768]
        r.cs[0:256], r.cs[256:512] = cos_v, cos_v
        r.sn[0:256], r.sn[256:512] = sin_v, sin_v
        row = lax.broadcasted_iota(jnp.int32, (512, 128), 0)
        lane = lax.broadcasted_iota(jnp.int32, (512, 128), 1)
        noisy = row < 256
        block = (row % 256) // 16
        first_blocks = r.lengths[0, 0]
        for h in range(2):
            col = lane - 64 * (1 - h)
            at = col % 16
            same = (block >= first_blocks) == (at >= first_blocks)
            clean_ok = same & ((at < block) | ((at == block) & ~noisy))
            ok = jnp.where(col < 16, clean_ok.astype(jnp.int32), (at == block).astype(jnp.int32))
            used = (col >= 0) & (col < 32)
            r.fq[h] = jnp.where(used & (ok == 0), NEG, 0.0).astype(BF)
            mine = jnp.where(noisy, block + 16, block)
            r.fk[h] = (used & (col == mine)).astype(BF)
        zero = jnp.zeros((128, 128), BF)
        for q in (0, 256):
            r.ds_c[0, q : q + 128, 128:256] = zero
            r.ds_c[1, q : q + 128, 128:256] = zero
            for head in range(6):
                r.ec[head, q : q + 128, 128:256] = zero

    @step
    def slot_order():
        w.wait(r.hid.at[oth], i0)
        for n in range(0, 768, 256):
            r.x[:, n : n + 256] = dot_tn(r.perm[...], r.hid[:, n : n + 256])

    @step
    def slot_order_grad():
        w.wait(r.dgiven.at[oth], i0 + 1)
        for n in range(0, 768, 256):
            r.dsl[:, n : n + 256] = dot_tn(r.perm[...], r.dgiven[:, n : n + 256]).astype(BF)
        r.dslT[...] = r.dsl[...].T
        r.grow[...] = jnp.sum(r.dsl[...].astype(F32), axis=0, keepdims=True)

    def norm(src_ref, n_ref, inv_ref, ln_ref, gain):
        def chunk(q):
            v = src_ref[q]
            cen = v - mean_of(v)
            inv = lax.rsqrt(mean_of(cen * cen) + EPS)
            nv = cen * inv
            n_ref[q] = nv
            inv_ref[q] = jnp.broadcast_to(inv, (64, 128))
            if ln_ref is not None:
                ln_ref[q] = (nv * r.vrow[gain : gain + 1]).astype(BF)

        rows_loop(chunk)

    @step
    def first_norm():
        norm(r.x, r.n1, r.inv1, None, 0)

    def ub_mask():
        d_of = lax.broadcasted_iota(jnp.int32, (384, 1536), 0)
        n_of = lax.broadcasted_iota(jnp.int32, (384, 1536), 1)
        spread = (
            lax.broadcasted_iota(jnp.int32, (128, 1536), 0)
            == 4 + lax.broadcasted_iota(jnp.int32, (128, 1536), 1) % 4
        ).astype(BF)
        return n_of // 4 == d_of, spread

    @step
    def vectors():
        r.vrow[...] = W[VEC].reshape(768, 128).astype(F32).T[0:8]

        def chunk(q):
            r.ln1[q] = (r.n1[q] * r.vrow[0:1]).astype(BF)

        rows_loop(chunk)

    first_all = lax.broadcasted_iota(jnp.int32, (512, 128), 1) < 64

    def qkv_step(i, tiles):
        def qkv():
            y = dot(r.ln1[...], wide(W, tiles))
            for k in range(len(tiles)):
                t = i + k
                v = y[:, 128 * k : 128 * k + 128].astype(BF)
                cols = slice(128 * (t % 3), 128 * (t % 3) + 128)
                if t >= 6:
                    one = jnp.ones_like(v)
                    r.v2[0, :, cols] = jnp.where(first_all, v, one)
                    r.v2[1, :, cols] = jnp.where(first_all, one, v)
                    continue
                f = v.astype(F32)
                f = (f * r.cs[...] + partner_lanes(f) * r.sn[...]).astype(BF)
                if t < 3:
                    f = f * 0.125
                to, fill = (r.q2, r.fq) if t < 3 else (r.k2, r.fk)
                to[0, :, cols] = jnp.where(first_all, f, fill[0])
                to[1, :, cols] = jnp.where(first_all, fill[1], f)

        return qkv

    for i, tiles in pairs_of(QKV):
        step(qkv_step(i, tiles))

    @step
    def up_bias():
        mask, spread = ub_mask()
        half_rows = W[VEC, pl.ds(2 * s, 2)].reshape(384, 128)
        r.ubrow[...] = jnp.sum(jnp.where(mask, dot(half_rows, spread), 0.0), axis=0, keepdims=True)

    lane = lax.broadcasted_iota(jnp.int32, (128, 128), 1)
    first = lane < 64

    def attend_step(p, blocks):
        def attend():
            cols = slice(128 * p, 128 * p + 128)
            items = [(slice(q0, q0 + 128), nc, k0, h) for q0, nc, k0 in blocks for h in range(2)]
            scores, outs = [], []
            for rows, nc, k0, h in items:
                q = r.q2[h, rows, cols]
                sc = dot_nt(q, r.k2[h, 256 : 256 + nc, cols])
                if k0 is not None:
                    sc = jnp.concatenate([sc, dot_nt(q, r.k2[h, k0 : k0 + 128, cols])], axis=1)
                scores.append(sc)
            tops = [jnp.max(sc, axis=1, keepdims=True) for sc in scores]
            exps = [jnp.exp(sc - top).astype(BF) for sc, top in zip(scores, tops)]
            for (rows, nc, k0, h), e in zip(items, exps):
                r.ec[2 * p + h, rows, 0:nc] = e[:, 0:nc]
                o = dot(e[:, 0:nc], r.v2[h, 256 : 256 + nc, cols])
                if k0 is not None:
                    r.en[2 * p + h, rows] = e[:, nc : nc + 128]
                    o = o + dot(e[:, nc : nc + 128], r.v2[h, k0 : k0 + 128, cols])
                outs.append(o)
            for i in range(0, len(items), 2):
                rows, one, two = items[i][0], outs[i], outs[i + 1]
                rec = 1.0 / jnp.where(first, pltpu.roll(one, 64, 1), pltpu.roll(two, 64, 1))
                r.rec[rows, cols] = rec
                r.att[rows, cols] = (jnp.where(first, one, two) * rec).astype(BF)

        return attend

    for p in range(3):
        step(attend_step(p, BLOCKS[:2]))
        step(attend_step(p, BLOCKS[2:]))

    @step
    def out_product():
        for n in range(0, 768, 256):
            y = dot_nt(r.att[...], wide(W, OUT, (n, n + 256)))
            r.part[:, n : n + 256] = y
            r.sendb[0, :, n : n + 256] = y.astype(BF)
        w.send(r.sendb.at[0], r.recvb.at[0], i0 + 2, other)

    @step
    def second_norm():
        w.wait(r.recvb.at[0], i0 + 2)

        def add_mid(q):
            r.middle[q] = r.x[q] + r.part[q] + r.recvb[0, q].astype(F32)

        rows_loop(add_mid)
        norm(r.middle, r.n2, r.inv2, r.ln2, 1)

    def up_step(i, tiles):
        def up():
            cols = slice(128 * i, 128 * i + 256)
            pre = dot(r.ln2[...], wide(W, tiles)) + r.ubrow[:, cols]
            sq = pre * pre
            th = jnp.tanh(0.7978845608028654 * (pre + 0.044715 * pre * sq))
            r.act[:, cols] = (0.5 * pre * (1.0 + th)).astype(BF)
            slope = 0.5 * (1.0 + th) + 0.5 * pre * (1.0 - th * th) * (
                0.7978845608028654 * (1.0 + 0.134145 * sq)
            )
            r.dgelu[i], r.dgelu[i + 1] = slope[:, 0:128], slope[:, 128:256]

        return up

    for i, tiles in pairs_of(UP):
        step(up_step(i, tiles))

    def store(tiles, y):
        for k, t in enumerate(tiles):
            G[t] = y[:, 128 * k : 128 * k + 128].astype(BF).reshape(4, 4, 48, 128)

    def weight_steps(name, tiles, leftT, right):
        def make(i, group):
            def fn():
                store(group, dot(leftT[...], right[:, 128 * i : 128 * (i + len(group))]))

            fn.__name__ = name
            return fn

        for i, group in pairs_of(tiles):
            step(make(i, group))

    weight_steps("grad_down", GDOWN, r.dslT, r.act)

    def down_back_step(i, tiles):
        def down_back():
            cols = slice(128 * i, 128 * i + 256)
            slope = jnp.concatenate([r.dgelu[i], r.dgelu[i + 1]], axis=1)
            g = (dot(r.dsl[...], wide(W, tiles)) * slope).astype(BF)
            r.gpre[:, cols] = g
            r.gub[:, cols] = jnp.sum(g.astype(F32), axis=0, keepdims=True)

        return down_back

    for i, tiles in pairs_of(DOWN):
        step(down_back_step(i, tiles))

    @step
    def up_back():
        for n in range(0, 768, 256):
            y = dot_nt(r.gpre[...], wide(W, UP, (n, n + 256)))
            r.part[:, n : n + 256] = y
            r.sendb[1, :, n : n + 256] = y.astype(BF)
        w.send(r.sendb.at[1], r.recvb.at[1], i0 + 3, other)

    @step
    def grad_vectors():
        rows = jnp.concatenate(
            [jnp.zeros((2, 768), F32), r.grow[...], jnp.zeros((125, 768), F32)], axis=0
        )
        G[GVEC] = rows.T.astype(BF).reshape(4, 4, 48, 128)
        mask, spread = ub_mask()
        ub = dot_nt(jnp.where(mask, r.gub[...], 0.0).astype(BF), spread)
        old = G[GVEC, pl.ds(2 * s, 2)].reshape(384, 128)
        G[GVEC, pl.ds(2 * s, 2)] = (old.astype(F32) + ub).astype(BF).reshape(2, 4, 48, 128)

    @step
    def lnb_t():
        r.lnbT[...] = r.ln2[...].T

    weight_steps("grad_up", GUP, r.lnbT, r.gpre)

    @step
    def middle_back():
        w.wait(r.recvb.at[1], i0 + 3)

        def mid_back(q):
            gl = r.part[q] + r.recvb[1, q].astype(F32)
            nv = r.n2[q]
            u = gl * r.vrow[1:2]
            g = r.dsl[q].astype(F32) + r.inv2[q][:, 0:1] * (u - mean_of(u) - nv * mean_of(u * nv))
            r.gm[q] = g
            r.gmb[q] = g.astype(BF)

        rows_loop(mid_back)

    @step
    def out_back():
        for i, tiles in pairs_of(OUT):
            r.gatt[:, 128 * i : 128 * (i + len(tiles))] = dot(r.gmb[...], wide(W, tiles)).astype(BF)

    @step
    def grad_out_t():
        r.gmT[...] = r.gmb[...].T

    weight_steps("grad_out", GOUT, r.gmT, r.att)

    def attend_prep_step(p):
        def attend_prep():
            cols = slice(128 * p, 128 * p + 128)
            ga = r.gatt[:, cols].astype(F32) * r.rec[:, cols]
            gb = ga.astype(BF)
            r.ga[:, cols] = gb
            t = gb.astype(F32) * r.att[:, cols].astype(F32)
            hi = t.astype(BF)
            lo = (t - hi.astype(F32)).astype(BF)
            li = lax.broadcasted_iota(jnp.int32, (128, 128), 0)
            lj = lax.broadcasted_iota(jnp.int32, (128, 128), 1)
            across = ((li < 64) != (lj < 64)).astype(BF)
            delta = -(dot(hi, across) + dot(lo, across))
            dh = delta.astype(BF)
            dl = (delta - dh.astype(F32)).astype(BF)
            ln = lax.broadcasted_iota(jnp.int32, (512, 128), 1) % 64
            fill = jnp.where(ln == 0, dh, jnp.where(ln == 1, dl, jnp.zeros_like(dh)))
            r.g2[0, :, cols] = jnp.where(first_all, gb, fill)
            r.g2[1, :, cols] = jnp.where(first_all, fill, gb)

        return attend_prep

    def attend_back_step(p, h):
        def attend_back():
            head = 2 * p + h
            cols = slice(128 * p, 128 * p + 128)
            items = [(slice(q0, q0 + 128), nc, k0) for q0, nc, k0 in BLOCKS]
            dps = []
            for rows, nc, k0 in items:
                g = r.g2[h, rows, cols]
                dp = dot_nt(g, r.v2[h, 256 : 256 + nc, cols])
                if k0 is not None:
                    dp = jnp.concatenate([dp, dot_nt(g, r.v2[h, k0 : k0 + 128, cols])], axis=1)
                dps.append(dp)
            ds = []
            for (rows, nc, k0), dp in zip(items, dps):
                e = r.ec[head, rows, 0:nc]
                if k0 is not None:
                    e = jnp.concatenate([e, r.en[head, rows]], axis=1)
                ds.append((e.astype(F32) * dp).astype(BF))
            for (rows, nc, k0), d in zip(items, ds):
                r.ds_c[h, rows, 0:nc] = d[:, 0:nc]
                o = dot(d[:, 0:nc], r.k2[h, 256 : 256 + nc, cols])
                if k0 is not None:
                    o = o + dot(d[:, nc : nc + 128], r.k2[h, k0 : k0 + 128, cols])
                    r.dk[h, rows] = dot_tn(d[:, nc : nc + 128], r.q2[h, rows, cols])
                    r.dv[h, rows] = dot_tn(r.en[head, rows], r.ga[rows, cols])
                r.dq[h, rows] = o
            r.dk[h, 256:512] = dot_tn(r.ds_c[h], r.q2[h, :, cols])
            r.dv[h, 256:512] = dot_tn(r.ec[head], r.ga[:, cols])

        return attend_back

    def attend_join_step(p):
        def attend_join():
            for i, (ref, scale) in enumerate(((r.dq, 0.125), (r.dk, 1.0))):
                v = jnp.where(first_all, ref[0], ref[1]) * scale
                v = v * r.cs[...] - partner_lanes(v) * r.sn[...]
                r.grows[:, 384 * i + 128 * p : 384 * i + 128 * p + 128] = v.astype(BF)
            v = jnp.where(first_all, r.dv[0], r.dv[1])
            r.grows[:, 768 + 128 * p : 768 + 128 * p + 128] = v.astype(BF)

        return attend_join

    for p in range(3):
        step(attend_prep_step(p))
        step(attend_back_step(p, 0))
        step(attend_back_step(p, 1))
        step(attend_join_step(p))

    @step
    def lna_t():
        r.lnaT[...] = r.ln1[...].T

    weight_steps("grad_qkv", GQKV, r.lnaT, r.grows)

    @step
    def qkv_back():
        for n in range(0, 768, 256):
            r.part[:, n : n + 256] = dot_nt(r.grows[...], wide(W, QKV, (n, n + 256)))

    @step
    def first_back():
        def chunk(q):
            gl = r.part[q]
            nv = r.n1[q]
            u = gl * r.vrow[0:1]
            r.part[q] = r.inv1[q][:, 0:1] * (u - mean_of(u) - nv * mean_of(u * nv))

        rows_loop(chunk)

    @step
    def hidden_other():
        r.half_out[0] = dot(r.perm[oth], r.part[...].astype(BF)).astype(BF)
        w.send(r.half_out.at[0], r.half_in.at[0], i0 + 4, other)

    def back_to_given(v):
        hi = v.astype(BF)
        lo = (v - hi.astype(F32)).astype(BF)
        return dot(r.perm[own], hi) + dot(r.perm[own], lo)

    @step
    def hidden_own():
        for n in range(0, 768, 256):
            r.grad_hidden[:, n : n + 256] = back_to_given(r.gm[:, n : n + 256] + r.part[:, n : n + 256])

    def down_product_step(n):
        def down_product():
            cols = slice(n, n + 256)
            y = dot_nt(r.act[...], wide(W, DOWN, (n, n + 256)))
            r.half_out[1, :, cols] = dot(r.perm[oth], y.astype(BF)).astype(BF)
            r.outp[:, cols] = back_to_given(y + r.middle[:, cols] + r.vrow[2:3, cols])
            if n == 512:
                w.send(r.half_out.at[1], r.half_in.at[1], i0 + 5, other)

        return down_product

    for n in (0, 256, 512):
        step(down_product_step(n))

    @step
    def outputs():
        w.wait(r.half_in.at[0], i0 + 4)
        r.grad_hidden[...] += r.half_in[0].astype(F32)
        w.wait(r.half_in.at[1], i0 + 5)
        r.output[...] = (r.outp[...] + r.half_in[1].astype(F32)).astype(BF)

    return steps


LAYER_BUFFERS = dict(
    hid=((512, 768), BF),
    dgiven=((512, 768), BF),
    perm=((512, 512), BF),
    x=((512, 768), F32),
    n1=((512, 768), F32),
    inv1=((512, 128), F32),
    ln1=((512, 768), BF),
    lnaT=((768, 512), BF),
    lnbT=((768, 512), BF),
    gmT=((768, 512), BF),
    dslT=((768, 512), BF),
    cs=((512, 128), F32),
    sn=((512, 128), F32),
    fq=((2, 512, 128), BF),
    fk=((2, 512, 128), BF),
    q2=((2, 512, 384), BF),
    k2=((2, 512, 384), BF),
    v2=((2, 512, 384), BF),
    ec=((6, 512, 256), BF),
    en=((6, 256, 128), BF),
    ds_c=((2, 512, 256), BF),
    rec=((512, 384), F32),
    ga=((512, 384), BF),
    g2=((2, 512, 384), BF),
    att=((512, 384), BF),
    part=((512, 768), F32),
    sendb=((2, 512, 768), BF),
    recvb=((2, 512, 768), BF),
    middle=((512, 768), F32),
    n2=((512, 768), F32),
    inv2=((512, 128), F32),
    act=((512, 1536), BF),
    dgelu=((12, 512, 128), F32),
    dsl=((512, 768), BF),
    gpre=((512, 1536), BF),
    gatt=((512, 384), BF),
    grows=((512, 1152), BF),
    outp=((256, 768), F32),
    half_in=((2, 256, 768), BF),
    half_out=((2, 256, 768), BF),
    vrow=((8, 768), F32),
    grow=((1, 768), F32),
    ubrow=((1, 1536), F32),
    gub=((1, 1536), F32),
)


def add_to(dst, *terms):
    total = dst[...].astype(F32)
    for t in terms:
        total = total + t[...].astype(F32)
    dst[...] = total.astype(BF)


def reduce_ring(w, block, halves, got, far, right, left, over, me, whole, direct):
    i0 = w.take(6)
    bl, br, bo = (me + 3) % 4, (me + 1) % 4, (me + 2) % 4

    def send_all():
        for i, (k, to) in enumerate(((br, right), (bl, left), (bo, over))):
            w.send(block(k), whole[i], i0 + i, to)

    def wait_all():
        for i in range(3):
            w.wait(whole[i], i0 + i)
        add_to(block(me), *whole)

    if direct:
        return [send_all, wait_all]
    (la, lb), (ra, rb) = got
    fl, fr = far

    def first():
        a, b = halves(bo)
        w.send(a, fl, i0, right)
        w.send(b, fr, i0 + 1, left)
        w.send(halves(br)[1], lb, i0 + 2, right)
        w.send(halves(bl)[0], ra, i0 + 3, left)

    def second():
        w.wait(fl, i0)
        a = halves(br)[0]
        add_to(a, fl)
        w.send(a, la, i0 + 4, right)
        w.wait(fr, i0 + 1)
        b = halves(bl)[1]
        add_to(b, fr)
        w.send(b, rb, i0 + 5, left)

    def third():
        a, b = halves(me)
        w.wait(lb, i0 + 2)
        w.wait(rb, i0 + 5)
        add_to(b, lb, rb)
        w.wait(ra, i0 + 3)
        w.wait(la, i0 + 4)
        add_to(a, la, ra)

    return [first, second, third]


def reduce_pairs(w, half, narrow, wide):
    c = w.c
    i0 = w.take(6)
    me, other = c.zl, 1 - c.zl

    def move(k, h, to, i, chip_id):
        w.send(half(k, h), to, i0 + i, chip_id)

    def got(k, h, ref, i):
        w.wait(ref, i0 + i)
        add_to(half(k, h), ref)

    def s0():
        move(c.kp, other, narrow(0), 0, c.zi)

    def s1():
        got(c.kp, me, narrow(0), 0)
        move(c.kp, me, narrow(1), 2, c.zo)
        move(c.kf, me, wide(0, me), 1, c.zi)

    def s2():
        got(c.kf, other, narrow(1), 2)
        move(c.kf, other, wide(0, other), 4, c.zi)

    def s3():
        got(c.ke, other, wide(0, other), 1)
        move(c.ke, other, wide(1, other), 3, c.zo)

    def s4():
        got(c.ke, me, wide(0, me), 4)
        move(c.ke, me, wide(1, me), 5, c.zo)

    def s5():
        got(c.zh, me, wide(1, me), 3)
        got(c.zh, other, wide(1, other), 5)

    return [s0, s1, s2, s3, s4, s5]


def reduce_relay(w, block, got, direct):
    c = w.c
    i0 = w.take(3)

    def send_all():
        for i, (k, to) in enumerate(((c.ke, c.zo), (c.kf, c.z2i), (c.kp, c.z3))):
            w.send(block(k), got[i], i0 + i, to)

    def wait_all():
        for i in range(3):
            w.wait(got[i], i0 + i)
        add_to(block(c.zh), *got)

    if direct:
        return [send_all, wait_all]

    def s0():
        w.send(block(c.kp), got[0], i0, c.zo)

    def s1():
        w.wait(got[0], i0)
        add_to(block(c.kf), got[0])
        w.send(block(c.kf), got[1], i0 + 1, c.zi)

    def s2():
        w.wait(got[1], i0 + 1)
        add_to(block(c.ke), got[1])
        w.send(block(c.ke), got[2], i0 + 2, c.zo)

    def s3():
        w.wait(got[2], i0 + 2)
        add_to(block(c.zh), got[2])

    return [s0, s1, s2, s3]


def reduce_events(c, w, r):
    G, events = r.G, {}

    def stage(st):
        dz, dx, dw = REDUCE.direct_z[st], REDUCE.direct_x[st], REDUCE.direct_wide[st]
        xa, xb = REDUCE.x(st)
        za, zb = REDUCE.z(st)
        nz = zb - za
        zm = (nz + 1) // 2

        def buf(name):
            return getattr(r, f"r{st}{name}")

        def sides(ref, cut):
            return [(ref.at[(i, slice(None), slice(0, cut))], ref.at[(i, slice(None), slice(cut, 2 * cut))]) for i in range(2)]

        bx, bxf, bxz = buf("x"), buf("xf"), buf("xz")
        x = chain(
            reduce_ring(
                w,
                lambda i: G.at[xa:xb, i],
                lambda i: (G.at[xa:xb, i, 0:2], G.at[xa:xb, i, 2:4]),
                sides(bx, 2),
                (bxf.at[0], bxf.at[1]),
                c.xr,
                c.xl,
                c.xo,
                c.x,
                [bx.at[i] for i in range(3)] if dw else None,
                dw,
            ),
            reduce_relay(w, lambda k: G.at[xa:xb, c.x, k], [bxz.at[i] for i in range(3)], dz),
        )
        bz, bzh, bzx = buf("z"), buf("zh"), buf("zx")
        z = chain(
            reduce_pairs(
                w,
                lambda k, h: G.at[za:zb, pl.ds(2 * h, 2), k],
                lambda i: bzh.at[i],
                lambda i, h: bz.at[i, :, pl.ds(2 * h, 2)],
            ),
            reduce_ring(
                w,
                lambda i: G.at[za:zb, i, c.zh],
                lambda i: (G.at[za : za + zm, i, c.zh], G.at[za + zm : zb, i, c.zh]),
                [(bzx.at[i, 0:zm], bzx.at[i, zm:nz]) for i in range(2)],
                (bzx.at[2, 0:zm], bzx.at[2, zm:nz]),
                c.xr,
                c.xl,
                c.xo,
                c.x,
                [bzx.at[i] for i in range(3)] if dx else None,
                dx,
            ),
        )
        mine = REDUCE.y(st, c.y)
        by, byf, byx, byxf, byz = buf("y"), buf("yf"), buf("yx"), buf("yxf"), buf("yz")
        y = chain(
            reduce_ring(
                w,
                lambda i: G.at[REDUCE.y(st, i)],
                lambda i: (G.at[REDUCE.y(st, i), 0:2], G.at[REDUCE.y(st, i), 2:4]),
                sides(by, 2),
                (byf.at[0], byf.at[1]),
                c.yr,
                c.yl,
                c.yo,
                c.y,
                [by.at[i] for i in range(3)] if dw else None,
                dw,
            ),
            reduce_ring(
                w,
                lambda i: G.at[mine, i],
                lambda i: (G.at[mine, i, 0:2], G.at[mine, i, 2:4]),
                sides(byx, 2),
                (byxf.at[0], byxf.at[1]),
                c.xr,
                c.xl,
                c.xo,
                c.x,
                [byx.at[i] for i in range(3)],
                True,
            ),
            reduce_relay(w, lambda k: G.at[mine, c.x, k], [byz.at[i] for i in range(3)], True),
        )

        def group(name, a, b):
            base = w.take(7)
            slab, held = buf("s" + name), buf("h" + name)

            def spread():
                row = lax.broadcasted_iota(jnp.int32, (64, 48), 0)
                col = lax.broadcasted_iota(jnp.int32, (64, 48), 1)
                pick = ((col // 6 == row // 8) & (col % 6 == row % 8)).astype(BF)
                for i in range(a, b):
                    o = dot(pick, G[REDUCE.tile(st, i, c.y), c.x, c.zh]).astype(BF)
                    slab[:, i - a] = o.reshape(8, 8, 128)
                for d in range(1, 8):
                    dm = (c.m + d) % 8
                    w.send(slab.at[dm], held.at[c.m], base + d - 1, c.f - c.m + dm)
                held[c.m] = slab[c.m]

            def collect():
                for d in range(1, 8):
                    w.wait(held.at[(c.m + 8 - d) % 8], base + d - 1)
                for i in range(a, b):
                    v = held[:, i - a].astype(F32)
                    if i < REDUCE.ny[st]:
                        for j in range(4):
                            r.done[c.s, REDUCE.tile(st, i, j)] = v[j] + v[j + 4]
                    else:
                        r.done[c.s, REDUCE.tile(st, i, 0)] = jnp.sum(v, axis=0)

            return [spread, collect]

        ny, nx = REDUCE.ny[st], REDUCE.nx[st]
        named(events, f"r{st}y", chain(y, group("y", 0, ny)))
        named(events, f"r{st}x", chain(x, group("x", ny, ny + nx)))
        named(events, f"r{st}z", chain(z, group("z", ny + nx, ny + nx + nz)))
        i0 = w.take(1)
        tiles = slice(REDUCE.first[st], REDUCE.first[st] + 4 * ny + nx + nz)

        def share():
            w.send(r.done.at[c.s, tiles], r.done.at[c.s, tiles], i0, {"seq": 1 - c.s})

        def shared():
            w.wait(r.done.at[1 - c.s, tiles], i0)

        named(events, f"r{st}d", [share, shared])

    for st in REDUCE.stages:
        stage(st)
    return events


def reduce_buffers():
    out = {}
    for st in REDUCE.stages:
        ny, nx, nz = REDUCE.ny[st], REDUCE.nx[st], REDUCE.nz[st]
        for name, dims in dict(
            x=(2 + REDUCE.direct_wide[st], nx, 4, 48, 128),
            xf=(2, nx, 2, 48, 128),
            xz=(3, nx, 48, 128),
            z=(2, nz, 4, 48, 128),
            zh=(2, nz, 2, 48, 128),
            zx=(3, nz, 48, 128),
            y=(2 + REDUCE.direct_wide[st], ny, 4, 4, 48, 128),
            yf=(2, ny, 2, 4, 48, 128),
            yx=(3, ny, 4, 48, 128),
            yxf=(2, ny, 2, 48, 128),
            yz=(3, ny, 48, 128),
            sx=(8, nx, 8, 128),
            hx=(8, nx, 8, 128),
            sy=(8, ny, 8, 128),
            hy=(8, ny, 8, 128),
            sz=(8, nz, 8, 128),
            hz=(8, nz, 8, 128),
        ).items():
            out[f"r{st}{name}"] = (dims, BF)
    return out


def rotary_table():
    freq = np.power(np.float32(10000.0), -2.0 * np.arange(32, dtype=np.float32) / np.float32(64))
    angle = np.arange(256, dtype=np.float32)[:, None] * freq.astype(np.float32)[None, :]
    cos, sin = np.cos(angle).astype(np.float32), np.sin(angle).astype(np.float32)
    terms = []
    for v in (np.concatenate([cos] * 4, axis=1), np.concatenate([-sin, sin] * 2, axis=1)):
        for _ in range(3):
            low = v.astype(BF)
            terms.append(low)
            v = v - low.astype(np.float32)
    return np.concatenate(terms, axis=1)


SCHEDULE = (
    77, 0, 1, 97, 2, 78, 3, 85, 90, 79, 98, 99, 110, 105, 91, 80, 86, 81, 106, 100, 111, 92, 87, 82, 107, 88, 93, 94,
    101, 112, 83, 89, 95, 102, 113, 114, 84, 108, 96, 4, 5, 6, 7, 8, 9, 10, 11, 12, 13, 115, 14, 15, 16, 17, 109, 63,
    103, 18, 116, 39, 104, 19, 20, 21, 22, 23, 24, 25, 26, 27, 28, 29, 30, 31, 32, 33, 34, 35, 36, 37, 38, 40, 41,
    42, 43, 44, 45, 117, 130, 123, 73, 46, 47, 48, 49, 50, 51, 52, 53, 54, 131, 55, 56, 57, 58, 59, 60, 61, 62, 118,
    64, 65, 66, 67, 68, 140, 153, 146, 124, 132, 133, 69, 70, 71, 72, 74, 75, 154, 134, 119, 147, 141, 125, 155, 156,
    142, 157, 76, 148, 120, 126, 135, 143, 149, 127, 121, 144, 158, 136, 150, 122, 128, 145, 159, 151, 137, 129, 138,
    152, 160, 161, 139, 162,
)

INPUTS = (
    "hidden", "d_out", "lengths", "source", "table", "qkv", "out", "up", "down",
    "gain_one", "gain_two", "down_bias", "up_bias",
)
OUTPUTS = ("output", "grad_hidden", "done")
BUFFERS = {
    "W": ((NT, 4, 4, 48, 128), BF),
    "G": ((NT, 4, 4, 48, 128), BF),
    **LAYER_BUFFERS,
    **gather_buffers(),
    **reduce_buffers(),
}
SEMS = 6 + 35 * len(GATHER.stages) + 58 * len(REDUCE.stages)


def step_kernel(*refs):
    r = Held()
    for name, ref in zip(INPUTS + OUTPUTS + tuple(BUFFERS), refs):
        setattr(r, name, ref)
    c = place()
    w = Wires(c, refs[-2], refs[-1])
    greeted = greet(c)
    events = {**layer_steps(c, w, r), **gather_events(c, w, r), **reduce_events(c, w, r)}
    fill_slab(c, r)
    events.pop("tables0")()
    pl.semaphore_wait(pltpu.get_barrier_semaphore(), greeted)
    steps = list(events.values())
    assert sorted(SCHEDULE) == list(range(len(steps)))
    for i in SCHEDULE:
        steps[i]()
    w.finish()


def finish_kernel(
    out_in, hidden_in, done, qkv, up, gain_one, gain_two, out, hidden, gqkv, gout, gup, gdown, g1, g2, gub, gdb, sems
):
    copies = [pltpu.make_async_copy(out_in, out, sems.at[0]), pltpu.make_async_copy(hidden_in, hidden, sems.at[1])]
    for copy in copies:
        copy.start()
    for core in range(2):
        for i, t in enumerate(GQKV):
            n = (i // 3) * 768 + core * 384 + (i % 3) * 128
            gqkv[:, n : n + 128] = done[core, t, 0:6]
        for tiles, ref, half in ((GOUT, gout, 384), (GUP, gup, 1536), (GDOWN, gdown, 1536)):
            for i, t in enumerate(tiles):
                n = core * half + i * 128
                ref[:, n : n + 128] = done[core, t, 0:6]
    lane = lax.broadcasted_iota(jnp.int32, (6, 128), 1)
    row = lax.broadcasted_iota(jnp.int32, (6, 128), 0)
    one = done[0, GVEC, 0:6]
    both = one + done[1, GVEC, 0:6]

    def as_row(places):
        total = jnp.zeros((6, 128), F32)
        for v, at in places:
            total = jnp.where(lane == at, v, total)
        return jnp.sum(total, axis=0)

    def gain_grad(weight, grad, gain):
        return jnp.sum(weight[...].astype(F32) * grad[...], axis=1, keepdims=True) / column(gain, 1, 0)

    g1[...] = as_row([(gain_grad(qkv, gqkv, gain_one), row)])[0:6]
    g2[...] = as_row([(gain_grad(up, gup, gain_two), row)])[0:6]
    gdb[...] = as_row([(one[:, 2:3], row)])[0:6]
    gub[...] = as_row([(both[:, 4 + k : 5 + k], 4 * row + k) for k in range(4)])[0:24]
    for copy in copies:
        copy.wait()


VM = pl.BlockSpec(memory_space=pltpu.VMEM)
ANY = pl.BlockSpec(memory_space=pl.ANY)
LIMIT = 62 * 2**20


def shape(dims, dtype=F32):
    return jax.ShapeDtypeStruct(dims, dtype)


def per_device(
    hidden, d_out, lengths, slot_source, first_gain, qkv_weight, out_weight, second_gain, up_weight, up_bias,
    down_weight, down_bias,
):
    parts = pl.pallas_call(
        step_kernel,
        out_shape=(shape((256, 768), BF), shape((256, 768)), shape((2, NT, 8, 128))),
        in_specs=[VM, VM, pl.BlockSpec(memory_space=pltpu.SMEM)] + [VM] * 10,
        out_specs=(VM,) * 3,
        scratch_shapes=[pltpu.VMEM(*v) for v in BUFFERS.values()] + [pltpu.SemaphoreType.DMA((SEMS,))] * 2,
        compiler_params=pltpu.CompilerParams(collective_id=0, has_side_effects=True, vmem_limit_bytes=LIMIT),
    )(
        hidden[0], d_out[0], lengths, slot_source, rotary_table(),
        qkv_weight, out_weight.T, up_weight, down_weight.T,
        first_gain[None], second_gain[None], down_bias[None], up_bias[None],
    )
    output, grad_hidden, gqkv, gout, gup, gdown, g1, g2, gub, gdb = pl.pallas_call(
        finish_kernel,
        out_shape=(
            shape((256, 768), BF),
            shape((256, 768)),
            shape((6, 2304)),
            shape((6, 768)),
            shape((6, 3072)),
            shape((6, 3072)),
            shape((6,)),
            shape((6,)),
            shape((24,)),
            shape((6,)),
        ),
        in_specs=[ANY] * 2 + [VM] * 5,
        out_specs=(ANY,) * 2 + (VM,) * 8,
        scratch_shapes=[pltpu.SemaphoreType.DMA((2,))],
    )(*parts, qkv_weight, up_weight, first_gain[None], second_gain[None])
    return (output[None], grad_hidden[None], g1, gqkv, gout.T, g2, gup, gub, gdown.T, gdb)


def solution(mesh):
    return jax.shard_map(
        per_device,
        mesh=mesh,
        in_specs=(
            P("fsdp", "seq", None),
            P("fsdp", "seq", None),
            P("fsdp", None),
            P("fsdp", None),
            P("fsdp"),
            P("fsdp", None),
            P(None, "fsdp"),
            P("fsdp"),
            P("fsdp", None),
            P("fsdp"),
            P(None, "fsdp"),
            P("fsdp"),
        ),
        out_specs=(
            P("fsdp", "seq", None),
            P("fsdp", "seq", None),
            P("fsdp"),
            P("fsdp", None),
            P(None, "fsdp"),
            P("fsdp"),
            P("fsdp", None),
            P("fsdp"),
            P(None, "fsdp"),
            P("fsdp"),
        ),
        check_vma=False,
    )
```

```python
import jax
import jax.numpy as jnp
import numpy as np
from jax import lax
from jax.experimental import pallas as pl
from jax.experimental.pallas import tpu as pltpu
from jax.sharding import PartitionSpec as P

MESH = pl.DeviceIdType.MESH
BF = jnp.bfloat16
F32 = jnp.float32
EPS = 1e-05
NEG = -1e30

NT = 37
VEC, QKV, OUT, UP, DOWN = 0, list(range(1, 10)), [10, 11, 12], list(range(13, 25)), list(range(25, 37))
GVEC, GQKV, GOUT, GUP, GDOWN = 24, list(range(28, 37)), [25, 26, 27], list(range(12, 24)), list(range(12))


class Split:
    def __init__(self, ny, nx, nz, direct_z, direct_x, direct_wide):
        self.ny, self.nx, self.nz = ny, nx, nz
        self.direct_z, self.direct_x, self.direct_wide = direct_z, direct_x, direct_wide
        self.stages = range(len(ny))
        self.first = [sum(4 * ny[i] + nx[i] + nz[i] for i in range(st)) for st in self.stages]
        self.slab = [ny[i] + nx[i] + nz[i] for i in self.stages]

    def x(self, st):
        a = self.first[st] + 4 * self.ny[st]
        return a, a + self.nx[st]

    def z(self, st):
        a = self.first[st] + 4 * self.ny[st] + self.nx[st]
        return a, a + self.nz[st]

    def y(self, st, j):
        return pl.ds(self.first[st] + j * self.ny[st], self.ny[st])

    def tile(self, st, i, y):
        if i < self.ny[st]:
            return self.first[st] + y * self.ny[st] + i
        return self.first[st] + 3 * self.ny[st] + i


GATHER = Split((1, 2), (5, 8), (4, 8), (0, 0), (1, 1), (0, 0))
REDUCE = Split((2, 1), (9, 4), (8, 4), (0, 0), (1, 1), (0, 0))


class Place:
    pass


def chip(x, z, y):
    return x * 32 + z * 4 + y


def place():
    c = Place()
    c.f = lax.axis_index("fsdp")
    c.s = lax.axis_index("seq")
    c.x = c.f // 32
    c.z = (c.f // 4) % 8
    c.y = c.f % 4
    c.zh = c.z // 2
    c.zl = c.z % 2
    c.m = c.f % 8
    sgn = 2 * c.zl - 1
    c.xr = chip((c.x + 1) % 4, c.z, c.y)
    c.xl = chip((c.x + 3) % 4, c.z, c.y)
    c.xo = chip((c.x + 2) % 4, c.z, c.y)
    c.yo = chip(c.x, c.z, (c.y + 2) % 4)
    c.yr = chip(c.x, c.z, (c.y + 1) % 4)
    c.yl = chip(c.x, c.z, (c.y + 3) % 4)
    c.zo = chip(c.x, (c.z + 8 + sgn) % 8, c.y)
    c.zi = chip(c.x, (c.z + 8 - sgn) % 8, c.y)
    c.z2 = chip(c.x, (c.z + 8 + 2 * sgn) % 8, c.y)
    c.z2i = chip(c.x, (c.z + 8 - 2 * sgn) % 8, c.y)
    c.z3 = chip(c.x, (c.z + 8 + 3 * sgn) % 8, c.y)
    c.ke = (c.zh + 4 + sgn) % 4
    c.kf = (c.zh + 4 - sgn) % 4
    c.kp = (c.zh + 2) % 4
    return c


def greet(c):
    sem = pltpu.get_barrier_semaphore()
    group = [c.f - c.m + (c.m + d) % 8 for d in range(1, 8)]
    devices = [c.xr, c.xl, c.xo, c.zo, c.z2, c.z2i, c.z3] + group
    for d in devices:
        pl.semaphore_signal(sem, inc=1, device_id={"fsdp": d}, device_id_type=MESH)
    pl.semaphore_signal(sem, inc=1, device_id={"seq": 1 - c.s}, device_id_type=MESH)
    return len(devices) + 1


class Wires:
    def __init__(self, c, send_sem, recv_sem):
        self.c, self.send_sem, self.recv_sem = c, send_sem, recv_sem
        self.used, self.pending = 0, []

    def take(self, n):
        self.used += n
        return self.used - n

    def copy(self, src, dst, i, to):
        return pltpu.make_async_remote_copy(
            src_ref=src,
            dst_ref=dst,
            send_sem=self.send_sem.at[i],
            recv_sem=self.recv_sem.at[i],
            device_id=to,
            device_id_type=MESH,
        )

    def send(self, src, dst, i, to):
        to = to if isinstance(to, dict) else {"fsdp": to}
        d = self.copy(src, dst, i, to)
        d.start()
        self.pending.append(d)

    def wait(self, dst, i):
        self.copy(dst, dst, i, {"fsdp": self.c.f}).wait_recv()

    def finish(self):
        for d in self.pending:
            d.wait_send()


def gather_ring(w, block, halves, right, left, far, me, direct):
    i0 = w.take(4)
    bl, br, bo = (me + 3) % 4, (me + 1) % 4, (me + 2) % 4

    def send_all():
        for i, to in enumerate((right, left, far)):
            w.send(block(me), block(me), i0 + i, to)

    def wait_all():
        for i, k in enumerate((bl, br, bo)):
            w.wait(block(k), i0 + i)

    if direct:
        return [send_all, wait_all]

    def first():
        w.send(block(me), block(me), i0, right)
        w.send(block(me), block(me), i0 + 1, left)

    def second():
        w.wait(block(bl), i0)
        a = halves(bl)[0]
        w.send(a, a, i0 + 2, right)
        w.wait(block(br), i0 + 1)
        b = halves(br)[1]
        w.send(b, b, i0 + 3, left)

    def third():
        a, b = halves(bo)
        w.wait(a, i0 + 2)
        w.wait(b, i0 + 3)

    return [first, second, third]


def gather_pairs(w, half):
    c = w.c
    i0 = w.take(6)
    me, other = c.zl, 1 - c.zl

    def move(k, h, i, to):
        w.send(half(k, h), half(k, h), i0 + i, to)

    def got(k, h, i):
        w.wait(half(k, h), i0 + i)

    def s0():
        move(c.zh, other, 0, c.zo)

    def s1():
        got(c.ke, me, 0)
        move(c.ke, me, 2, c.zi)
        move(c.zh, me, 1, c.zo)

    def s2():
        got(c.kf, other, 2)
        move(c.kf, other, 4, c.zo)

    def s3():
        got(c.ke, other, 1)
        move(c.ke, other, 3, c.zi)

    def s4():
        got(c.kp, me, 4)
        move(c.kp, me, 5, c.zi)

    def s5():
        got(c.kf, me, 3)
        got(c.kp, other, 5)

    return [s0, s1, s2, s3, s4, s5]


def gather_relay(w, block, direct):
    c = w.c
    i0 = w.take(3)

    def send_all():
        for i, to in enumerate((c.zo, c.z2, c.z3)):
            w.send(block(c.zh), block(c.zh), i0 + i, to)

    def wait_all():
        for i, k in enumerate((c.ke, c.kf, c.kp)):
            w.wait(block(k), i0 + i)

    if direct:
        return [send_all, wait_all]

    def s0():
        w.send(block(c.zh), block(c.zh), i0, c.zo)

    def s1():
        w.wait(block(c.ke), i0)
        w.send(block(c.ke), block(c.ke), i0 + 1, c.zi)

    def s2():
        w.wait(block(c.kf), i0 + 1)
        w.send(block(c.kf), block(c.kf), i0 + 2, c.zo)

    def s3():
        w.wait(block(c.kp), i0 + 2)

    return [s0, s1, s2, s3]


def chain(*parts):
    steps = list(parts[0])
    for part in parts[1:]:
        last, then = steps.pop(), part[0]

        def both(last=last, then=then):
            last()
            then()

        steps += [both, *part[1:]]
    return steps


def named(events, name, steps):
    for i, fn in enumerate(steps):
        events[f"{name}{i}"] = fn


def gather_events(c, w, r):
    W, events = r.W, {}

    def stage(st):
        base = w.take(7)
        slab, held = getattr(r, f"gs{st}"), getattr(r, f"gh{st}")

        def start():
            for d in range(1, 8):
                dm = (c.m + d) % 8
                w.send(slab.at[dm % 4], held.at[c.m], base + d - 1, c.f - c.m + dm)
            held[c.m] = slab[c.y]

        def align():
            for d in range(1, 8):
                w.wait(held.at[(c.m + 8 - d) % 8], base + d - 1)
            row = lax.broadcasted_iota(jnp.int32, (48, 64), 0)
            col = lax.broadcasted_iota(jnp.int32, (48, 64), 1)
            pick = ((row // 6 == col // 8) & (row % 6 == col % 8)).astype(BF)
            for i in range(GATHER.slab[st]):
                v = held[:, i].reshape(64, 128)
                W[GATHER.tile(st, i, c.y), c.x, c.zh] = dot(pick, v).astype(BF)

        events[f"g{st}s"], events[f"g{st}a"] = start, align
        dz, dx, dw = GATHER.direct_z[st], GATHER.direct_x[st], GATHER.direct_wide[st]
        xa, xb = GATHER.x(st)
        za, zb = GATHER.z(st)
        zm = (za + zb + 1) // 2
        x = chain(
            gather_relay(w, lambda k: W.at[xa:xb, c.x, k], dz),
            gather_ring(
                w,
                lambda i: W.at[xa:xb, i],
                lambda i: (W.at[xa:xb, i, 0:2], W.at[xa:xb, i, 2:4]),
                c.xr,
                c.xl,
                c.xo,
                c.x,
                dw,
            ),
        )
        z = chain(
            gather_ring(
                w,
                lambda i: W.at[za:zb, i, c.zh],
                lambda i: (W.at[za:zm, i, c.zh], W.at[zm:zb, i, c.zh]),
                c.xr,
                c.xl,
                c.xo,
                c.x,
                dx,
            ),
            gather_pairs(w, lambda k, h: W.at[za:zb, pl.ds(2 * h, 2), k]),
        )
        mine = GATHER.y(st, c.y)
        y = chain(
            gather_relay(w, lambda k: W.at[mine, c.x, k], True),
            gather_ring(
                w,
                lambda i: W.at[mine, i],
                lambda i: (W.at[mine, i, 0:2], W.at[mine, i, 2:4]),
                c.xr,
                c.xl,
                c.xo,
                c.x,
                True,
            ),
            gather_ring(
                w,
                lambda i: W.at[GATHER.y(st, i)],
                lambda i: (W.at[GATHER.y(st, i), 0:2], W.at[GATHER.y(st, i), 2:4]),
                c.yr,
                c.yl,
                c.yo,
                c.y,
                dw,
            ),
        )
        named(events, f"g{st}x", x)
        named(events, f"g{st}y", y)
        named(events, f"g{st}z", z)

    for st in GATHER.stages:
        stage(st)
    return events


def gather_buffers():
    out = {}
    for st in GATHER.stages:
        out[f"gs{st}"] = ((4, GATHER.slab[st], 8, 128), BF)
        out[f"gh{st}"] = ((8, GATHER.slab[st], 8, 128), BF)
    return out


def column(ref, step, first):
    lane = lax.broadcasted_iota(jnp.int32, (6, 6 * step), 1)
    row = lax.broadcasted_iota(jnp.int32, (6, 6 * step), 0)
    values = jnp.broadcast_to(ref[...].astype(F32), (6, 6 * step))
    return jnp.sum(jnp.where(lane == step * row + first, values, 0.0), axis=1, keepdims=True)


def fill_slab(c, r):
    zero = jnp.zeros((2, 128), BF)

    def vectors():
        lane = lax.broadcasted_iota(jnp.int32, (6, 128), 1)
        total = jnp.zeros((6, 128), F32)
        for col, ref in ((0, r.gain_one), (1, r.gain_two), (2, r.down_bias)):
            total = jnp.where(lane == col, column(ref, 1, 0), total)
        for k in range(4):
            total = jnp.where(lane == 4 + k, column(r.up_bias, 4, k), total)
        return total.astype(BF)

    def tile(n):
        if n == VEC:
            return vectors()
        if n < 10:
            part, i = (n - 1) // 3, (n - 1) % 3
            return r.qkv[:, pl.ds(pl.multiple_of(part * 768 + c.s * 384 + i * 128, 128), 128)]
        if n < 13:
            return r.out[:, pl.ds(pl.multiple_of(c.s * 384 + (n - 10) * 128, 128), 128)]
        ref, i = (r.up, n - 13) if n < 25 else (r.down, n - 25)
        return ref[:, pl.ds(pl.multiple_of(c.s * 1536 + i * 128, 128), 128)]

    for st in GATHER.stages:
        slab = getattr(r, f"gs{st}")
        for i in range(GATHER.slab[st]):
            for j in range(4):
                if i < GATHER.ny[st] or j == 0:
                    v = tile(GATHER.tile(st, i, j))
                slab[j, i, 0:6] = v
                slab[j, i, 6:8] = zero


def rows_loop(fn, size=64):
    def body(i, carry):
        fn(pl.ds(pl.multiple_of(i * size, size), size))
        return carry

    lax.fori_loop(0, 512 // size, body, 0)


def dot(a, b):
    return jnp.dot(a, b, preferred_element_type=F32)


def dot_nt(a, b):
    return lax.dot_general(a, b, (((1,), (1,)), ((), ())), preferred_element_type=F32)


def dot_tn(a, b):
    return lax.dot_general(a, b, (((0,), (0,)), ((), ())), preferred_element_type=F32)


def wide(W, tiles, rows=None):
    parts = []
    for t in tiles:
        v = W[t].reshape(768, 128)
        parts.append(v if rows is None else v[rows[0] : rows[1]])
    return parts[0] if len(parts) == 1 else jnp.concatenate(parts, axis=1)


def pairs_of(tiles):
    return [(i, tiles[i : i + 2]) for i in range(0, len(tiles), 2)]


def partner_lanes(v):
    lane = lax.broadcasted_iota(jnp.int32, v.shape, 1) % 64
    return jnp.where(lane < 32, pltpu.roll(v, 96, 1), pltpu.roll(v, 32, 1))


def mean_of(v):
    return jnp.sum(v, axis=1, keepdims=True) * (1.0 / 768.0)


BLOCKS = ((0, 128, 0), (128, 256, 128), (256, 128, None), (384, 256, None))


class Held:
    pass


def layer_steps(c, w, r):
    s = c.s
    other = {"seq": 1 - s}
    own = pl.ds(pl.multiple_of(s * 256, 256), 256)
    oth = pl.ds(pl.multiple_of(256 - s * 256, 256), 256)
    i0 = w.take(6)
    W, G = r.W, r.G
    r.gm, r.gmb, r.ln2 = r.x, r.hid, r.dgiven
    r.dq, r.dk, r.dv = r.dgelu.at[0:2], r.dgelu.at[2:4], r.dgelu.at[4:6]
    steps = {}

    def step(fn):
        name = fn.__name__
        steps[f"{name}{sum(k.rstrip('0123456789') == name for k in steps)}"] = fn

    @step
    def exchange_rows():
        w.send(r.hidden, r.hid.at[own], i0, other)
        w.send(r.d_out, r.dgiven.at[own], i0 + 1, other)
        r.hid[own] = r.hidden[...]
        r.dgiven[own] = r.d_out[...]

    @step
    def tables():
        src = r.source[...]
        r.perm[...] = (lax.broadcasted_iota(jnp.int32, (512, 512), 0) == src).astype(BF)
        first_len = r.lengths[0, 0] * 16
        token = lax.broadcasted_iota(jnp.int32, (256, 256), 0)
        offset = jnp.where(token >= first_len, token - first_len, token)
        at_pos = (lax.broadcasted_iota(jnp.int32, (256, 256), 1) == offset).astype(BF)
        parts = dot(at_pos, r.table[...])
        cos_v = parts[:, 0:128] + parts[:, 128:256] + parts[:, 256:384]
        sin_v = parts[:, 384:512] + parts[:, 512:640] + parts[:, 640:768]
        r.cs[0:256], r.cs[256:512] = cos_v, cos_v
        r.sn[0:256], r.sn[256:512] = sin_v, sin_v
        row = lax.broadcasted_iota(jnp.int32, (512, 128), 0)
        lane = lax.broadcasted_iota(jnp.int32, (512, 128), 1)
        noisy = row < 256
        block = (row % 256) // 16
        first_blocks = r.lengths[0, 0]
        for h in range(2):
            col = lane - 64 * (1 - h)
            at = col % 16
            same = (block >= first_blocks) == (at >= first_blocks)
            clean_ok = same & ((at < block) | ((at == block) & ~noisy))
            ok = jnp.where(col < 16, clean_ok.astype(jnp.int32), (at == block).astype(jnp.int32))
            used = (col >= 0) & (col < 32)
            r.fq[h] = jnp.where(used & (ok == 0), NEG, 0.0).astype(BF)
            mine = jnp.where(noisy, block + 16, block)
            r.fk[h] = (used & (col == mine)).astype(BF)
        zero = jnp.zeros((128, 128), BF)
        for q in (0, 256):
            r.ds_c[0, q : q + 128, 128:256] = zero
            r.ds_c[1, q : q + 128, 128:256] = zero
            for head in range(6):
                r.ec[head, q : q + 128, 128:256] = zero

    @step
    def slot_order():
        w.wait(r.hid.at[oth], i0)
        for n in range(0, 768, 256):
            r.x[:, n : n + 256] = dot_tn(r.perm[...], r.hid[:, n : n + 256])

    @step
    def slot_order_grad():
        w.wait(r.dgiven.at[oth], i0 + 1)
        for n in range(0, 768, 256):
            r.dsl[:, n : n + 256] = dot_tn(r.perm[...], r.dgiven[:, n : n + 256]).astype(BF)
        r.dslT[...] = r.dsl[...].T
        r.grow[...] = jnp.sum(r.dsl[...].astype(F32), axis=0, keepdims=True)

    def norm(src_ref, n_ref, inv_ref, ln_ref, gain):
        def chunk(q):
            v = src_ref[q]
            cen = v - mean_of(v)
            inv = lax.rsqrt(mean_of(cen * cen) + EPS)
            nv = cen * inv
            n_ref[q] = nv
            inv_ref[q] = jnp.broadcast_to(inv, (64, 128))
            if ln_ref is not None:
                ln_ref[q] = (nv * r.vrow[gain : gain + 1]).astype(BF)

        rows_loop(chunk)

    @step
    def first_norm():
        norm(r.x, r.n1, r.inv1, None, 0)

    def ub_mask():
        d_of = lax.broadcasted_iota(jnp.int32, (384, 1536), 0)
        n_of = lax.broadcasted_iota(jnp.int32, (384, 1536), 1)
        spread = (
            lax.broadcasted_iota(jnp.int32, (128, 1536), 0)
            == 4 + lax.broadcasted_iota(jnp.int32, (128, 1536), 1) % 4
        ).astype(BF)
        return n_of // 4 == d_of, spread

    @step
    def vectors():
        r.vrow[...] = W[VEC].reshape(768, 128).astype(F32).T[0:8]

        def chunk(q):
            r.ln1[q] = (r.n1[q] * r.vrow[0:1]).astype(BF)

        rows_loop(chunk)

    first_all = lax.broadcasted_iota(jnp.int32, (512, 128), 1) < 64

    def qkv_step(i, tiles):
        def qkv():
            y = dot(r.ln1[...], wide(W, tiles))
            for k in range(len(tiles)):
                t = i + k
                v = y[:, 128 * k : 128 * k + 128].astype(BF)
                cols = slice(128 * (t % 3), 128 * (t % 3) + 128)
                if t >= 6:
                    one = jnp.ones_like(v)
                    r.v2[0, :, cols] = jnp.where(first_all, v, one)
                    r.v2[1, :, cols] = jnp.where(first_all, one, v)
                    continue
                f = v.astype(F32)
                f = (f * r.cs[...] + partner_lanes(f) * r.sn[...]).astype(BF)
                if t < 3:
                    f = f * 0.125
                to, fill = (r.q2, r.fq) if t < 3 else (r.k2, r.fk)
                to[0, :, cols] = jnp.where(first_all, f, fill[0])
                to[1, :, cols] = jnp.where(first_all, fill[1], f)

        return qkv

    for i, tiles in pairs_of(QKV):
        step(qkv_step(i, tiles))

    @step
    def up_bias():
        mask, spread = ub_mask()
        half_rows = W[VEC, pl.ds(2 * s, 2)].reshape(384, 128)
        r.ubrow[...] = jnp.sum(jnp.where(mask, dot(half_rows, spread), 0.0), axis=0, keepdims=True)

    lane = lax.broadcasted_iota(jnp.int32, (128, 128), 1)
    first = lane < 64

    def attend_step(p, blocks):
        def attend():
            cols = slice(128 * p, 128 * p + 128)
            items = [(slice(q0, q0 + 128), nc, k0, h) for q0, nc, k0 in blocks for h in range(2)]
            scores, outs = [], []
            for rows, nc, k0, h in items:
                q = r.q2[h, rows, cols]
                sc = dot_nt(q, r.k2[h, 256 : 256 + nc, cols])
                if k0 is not None:
                    sc = jnp.concatenate([sc, dot_nt(q, r.k2[h, k0 : k0 + 128, cols])], axis=1)
                scores.append(sc)
            tops = [jnp.max(sc, axis=1, keepdims=True) for sc in scores]
            exps = [jnp.exp(sc - top).astype(BF) for sc, top in zip(scores, tops)]
            for (rows, nc, k0, h), e in zip(items, exps):
                r.ec[2 * p + h, rows, 0:nc] = e[:, 0:nc]
                o = dot(e[:, 0:nc], r.v2[h, 256 : 256 + nc, cols])
                if k0 is not None:
                    r.en[2 * p + h, rows] = e[:, nc : nc + 128]
                    o = o + dot(e[:, nc : nc + 128], r.v2[h, k0 : k0 + 128, cols])
                outs.append(o)
            for i in range(0, len(items), 2):
                rows, one, two = items[i][0], outs[i], outs[i + 1]
                rec = 1.0 / jnp.where(first, pltpu.roll(one, 64, 1), pltpu.roll(two, 64, 1))
                r.rec[rows, cols] = rec
                r.att[rows, cols] = (jnp.where(first, one, two) * rec).astype(BF)

        return attend

    for p in range(3):
        step(attend_step(p, BLOCKS[:2]))
        step(attend_step(p, BLOCKS[2:]))

    @step
    def out_product():
        for n in range(0, 768, 256):
            y = dot_nt(r.att[...], wide(W, OUT, (n, n + 256)))
            r.part[:, n : n + 256] = y
            r.sendb[0, :, n : n + 256] = y.astype(BF)
        w.send(r.sendb.at[0], r.recvb.at[0], i0 + 2, other)

    @step
    def second_norm():
        w.wait(r.recvb.at[0], i0 + 2)

        def add_mid(q):
            r.middle[q] = r.x[q] + r.part[q] + r.recvb[0, q].astype(F32)

        rows_loop(add_mid)
        norm(r.middle, r.n2, r.inv2, r.ln2, 1)

    def up_step(i, tiles):
        def up():
            cols = slice(128 * i, 128 * i + 256)
            pre = dot(r.ln2[...], wide(W, tiles)) + r.ubrow[:, cols]
            sq = pre * pre
            th = jnp.tanh(0.7978845608028654 * (pre + 0.044715 * pre * sq))
            r.act[:, cols] = (0.5 * pre * (1.0 + th)).astype(BF)
            slope = 0.5 * (1.0 + th) + 0.5 * pre * (1.0 - th * th) * (
                0.7978845608028654 * (1.0 + 0.134145 * sq)
            )
            r.dgelu[i], r.dgelu[i + 1] = slope[:, 0:128], slope[:, 128:256]

        return up

    for i, tiles in pairs_of(UP):
        step(up_step(i, tiles))

    def store(tiles, y):
        for k, t in enumerate(tiles):
            G[t] = y[:, 128 * k : 128 * k + 128].astype(BF).reshape(4, 4, 48, 128)

    def weight_steps(name, tiles, leftT, right):
        def make(i, group):
            def fn():
                store(group, dot(leftT[...], right[:, 128 * i : 128 * (i + len(group))]))

            fn.__name__ = name
            return fn

        for i, group in pairs_of(tiles):
            step(make(i, group))

    weight_steps("grad_down", GDOWN, r.dslT, r.act)

    def down_back_step(i, tiles):
        def down_back():
            cols = slice(128 * i, 128 * i + 256)
            slope = jnp.concatenate([r.dgelu[i], r.dgelu[i + 1]], axis=1)
            g = (dot(r.dsl[...], wide(W, tiles)) * slope).astype(BF)
            r.gpre[:, cols] = g
            r.gub[:, cols] = jnp.sum(g.astype(F32), axis=0, keepdims=True)

        return down_back

    for i, tiles in pairs_of(DOWN):
        step(down_back_step(i, tiles))

    @step
    def up_back():
        for n in range(0, 768, 256):
            y = dot_nt(r.gpre[...], wide(W, UP, (n, n + 256)))
            r.part[:, n : n + 256] = y
            r.sendb[1, :, n : n + 256] = y.astype(BF)
        w.send(r.sendb.at[1], r.recvb.at[1], i0 + 3, other)

    @step
    def grad_vectors():
        rows = jnp.concatenate(
            [jnp.zeros((2, 768), F32), r.grow[...], jnp.zeros((125, 768), F32)], axis=0
        )
        G[GVEC] = rows.T.astype(BF).reshape(4, 4, 48, 128)
        mask, spread = ub_mask()
        ub = dot_nt(jnp.where(mask, r.gub[...], 0.0).astype(BF), spread)
        old = G[GVEC, pl.ds(2 * s, 2)].reshape(384, 128)
        G[GVEC, pl.ds(2 * s, 2)] = (old.astype(F32) + ub).astype(BF).reshape(2, 4, 48, 128)

    @step
    def lnb_t():
        r.lnbT[...] = r.ln2[...].T

    weight_steps("grad_up", GUP, r.lnbT, r.gpre)

    @step
    def middle_back():
        w.wait(r.recvb.at[1], i0 + 3)

        def mid_back(q):
            gl = r.part[q] + r.recvb[1, q].astype(F32)
            nv = r.n2[q]
            u = gl * r.vrow[1:2]
            g = r.dsl[q].astype(F32) + r.inv2[q][:, 0:1] * (u - mean_of(u) - nv * mean_of(u * nv))
            r.gm[q] = g
            r.gmb[q] = g.astype(BF)

        rows_loop(mid_back)

    @step
    def out_back():
        for i, tiles in pairs_of(OUT):
            r.gatt[:, 128 * i : 128 * (i + len(tiles))] = dot(r.gmb[...], wide(W, tiles)).astype(BF)

    @step
    def grad_out_t():
        r.gmT[...] = r.gmb[...].T

    weight_steps("grad_out", GOUT, r.gmT, r.att)

    def attend_prep_step(p):
        def attend_prep():
            cols = slice(128 * p, 128 * p + 128)
            ga = r.gatt[:, cols].astype(F32) * r.rec[:, cols]
            gb = ga.astype(BF)
            r.ga[:, cols] = gb
            t = gb.astype(F32) * r.att[:, cols].astype(F32)
            hi = t.astype(BF)
            lo = (t - hi.astype(F32)).astype(BF)
            li = lax.broadcasted_iota(jnp.int32, (128, 128), 0)
            lj = lax.broadcasted_iota(jnp.int32, (128, 128), 1)
            across = ((li < 64) != (lj < 64)).astype(BF)
            delta = -(dot(hi, across) + dot(lo, across))
            dh = delta.astype(BF)
            dl = (delta - dh.astype(F32)).astype(BF)
            ln = lax.broadcasted_iota(jnp.int32, (512, 128), 1) % 64
            fill = jnp.where(ln == 0, dh, jnp.where(ln == 1, dl, jnp.zeros_like(dh)))
            r.g2[0, :, cols] = jnp.where(first_all, gb, fill)
            r.g2[1, :, cols] = jnp.where(first_all, fill, gb)

        return attend_prep

    def attend_back_step(p, h):
        def attend_back():
            head = 2 * p + h
            cols = slice(128 * p, 128 * p + 128)
            items = [(slice(q0, q0 + 128), nc, k0) for q0, nc, k0 in BLOCKS]
            dps = []
            for rows, nc, k0 in items:
                g = r.g2[h, rows, cols]
                dp = dot_nt(g, r.v2[h, 256 : 256 + nc, cols])
                if k0 is not None:
                    dp = jnp.concatenate([dp, dot_nt(g, r.v2[h, k0 : k0 + 128, cols])], axis=1)
                dps.append(dp)
            ds = []
            for (rows, nc, k0), dp in zip(items, dps):
                e = r.ec[head, rows, 0:nc]
                if k0 is not None:
                    e = jnp.concatenate([e, r.en[head, rows]], axis=1)
                ds.append((e.astype(F32) * dp).astype(BF))
            for (rows, nc, k0), d in zip(items, ds):
                r.ds_c[h, rows, 0:nc] = d[:, 0:nc]
                o = dot(d[:, 0:nc], r.k2[h, 256 : 256 + nc, cols])
                if k0 is not None:
                    o = o + dot(d[:, nc : nc + 128], r.k2[h, k0 : k0 + 128, cols])
                    r.dk[h, rows] = dot_tn(d[:, nc : nc + 128], r.q2[h, rows, cols])
                    r.dv[h, rows] = dot_tn(r.en[head, rows], r.ga[rows, cols])
                r.dq[h, rows] = o
            r.dk[h, 256:512] = dot_tn(r.ds_c[h], r.q2[h, :, cols])
            r.dv[h, 256:512] = dot_tn(r.ec[head], r.ga[:, cols])

        return attend_back

    def attend_join_step(p):
        def attend_join():
            for i, (ref, scale) in enumerate(((r.dq, 0.125), (r.dk, 1.0))):
                v = jnp.where(first_all, ref[0], ref[1]) * scale
                v = v * r.cs[...] - partner_lanes(v) * r.sn[...]
                r.grows[:, 384 * i + 128 * p : 384 * i + 128 * p + 128] = v.astype(BF)
            v = jnp.where(first_all, r.dv[0], r.dv[1])
            r.grows[:, 768 + 128 * p : 768 + 128 * p + 128] = v.astype(BF)

        return attend_join

    for p in range(3):
        step(attend_prep_step(p))
        step(attend_back_step(p, 0))
        step(attend_back_step(p, 1))
        step(attend_join_step(p))

    @step
    def lna_t():
        r.lnaT[...] = r.ln1[...].T

    weight_steps("grad_qkv", GQKV, r.lnaT, r.grows)

    @step
    def qkv_back():
        for n in range(0, 768, 256):
            r.part[:, n : n + 256] = dot_nt(r.grows[...], wide(W, QKV, (n, n + 256)))

    @step
    def first_back():
        def chunk(q):
            gl = r.part[q]
            nv = r.n1[q]
            u = gl * r.vrow[0:1]
            r.part[q] = r.inv1[q][:, 0:1] * (u - mean_of(u) - nv * mean_of(u * nv))

        rows_loop(chunk)

    @step
    def hidden_other():
        r.half_out[0] = dot(r.perm[oth], r.part[...].astype(BF)).astype(BF)
        w.send(r.half_out.at[0], r.half_in.at[0], i0 + 4, other)

    def back_to_given(v):
        hi = v.astype(BF)
        lo = (v - hi.astype(F32)).astype(BF)
        return dot(r.perm[own], hi) + dot(r.perm[own], lo)

    @step
    def hidden_own():
        for n in range(0, 768, 256):
            r.grad_hidden[:, n : n + 256] = back_to_given(r.gm[:, n : n + 256] + r.part[:, n : n + 256])

    def down_product_step(n):
        def down_product():
            cols = slice(n, n + 256)
            y = dot_nt(r.act[...], wide(W, DOWN, (n, n + 256)))
            r.half_out[1, :, cols] = dot(r.perm[oth], y.astype(BF)).astype(BF)
            r.outp[:, cols] = back_to_given(y + r.middle[:, cols] + r.vrow[2:3, cols])
            if n == 512:
                w.send(r.half_out.at[1], r.half_in.at[1], i0 + 5, other)

        return down_product

    for n in (0, 256, 512):
        step(down_product_step(n))

    @step
    def outputs():
        w.wait(r.half_in.at[0], i0 + 4)
        r.grad_hidden[...] += r.half_in[0].astype(F32)
        w.wait(r.half_in.at[1], i0 + 5)
        r.output[...] = (r.outp[...] + r.half_in[1].astype(F32)).astype(BF)

    return steps


LAYER_BUFFERS = dict(
    hid=((512, 768), BF),
    dgiven=((512, 768), BF),
    perm=((512, 512), BF),
    x=((512, 768), F32),
    n1=((512, 768), F32),
    inv1=((512, 128), F32),
    ln1=((512, 768), BF),
    lnaT=((768, 512), BF),
    lnbT=((768, 512), BF),
    gmT=((768, 512), BF),
    dslT=((768, 512), BF),
    cs=((512, 128), F32),
    sn=((512, 128), F32),
    fq=((2, 512, 128), BF),
    fk=((2, 512, 128), BF),
    q2=((2, 512, 384), BF),
    k2=((2, 512, 384), BF),
    v2=((2, 512, 384), BF),
    ec=((6, 512, 256), BF),
    en=((6, 256, 128), BF),
    ds_c=((2, 512, 256), BF),
    rec=((512, 384), F32),
    ga=((512, 384), BF),
    g2=((2, 512, 384), BF),
    att=((512, 384), BF),
    part=((512, 768), F32),
    sendb=((2, 512, 768), BF),
    recvb=((2, 512, 768), BF),
    middle=((512, 768), F32),
    n2=((512, 768), F32),
    inv2=((512, 128), F32),
    act=((512, 1536), BF),
    dgelu=((12, 512, 128), F32),
    dsl=((512, 768), BF),
    gpre=((512, 1536), BF),
    gatt=((512, 384), BF),
    grows=((512, 1152), BF),
    outp=((256, 768), F32),
    half_in=((2, 256, 768), BF),
    half_out=((2, 256, 768), BF),
    vrow=((8, 768), F32),
    grow=((1, 768), F32),
    ubrow=((1, 1536), F32),
    gub=((1, 1536), F32),
)


def add_to(dst, *terms):
    total = dst[...].astype(F32)
    for t in terms:
        total = total + t[...].astype(F32)
    dst[...] = total.astype(BF)


def reduce_ring(w, block, halves, got, far, right, left, over, me, whole, direct):
    i0 = w.take(6)
    bl, br, bo = (me + 3) % 4, (me + 1) % 4, (me + 2) % 4

    def send_all():
        for i, (k, to) in enumerate(((br, right), (bl, left), (bo, over))):
            w.send(block(k), whole[i], i0 + i, to)

    def wait_all():
        for i in range(3):
            w.wait(whole[i], i0 + i)
        add_to(block(me), *whole)

    if direct:
        return [send_all, wait_all]
    (la, lb), (ra, rb) = got
    fl, fr = far

    def first():
        a, b = halves(bo)
        w.send(a, fl, i0, right)
        w.send(b, fr, i0 + 1, left)
        w.send(halves(br)[1], lb, i0 + 2, right)
        w.send(halves(bl)[0], ra, i0 + 3, left)

    def second():
        w.wait(fl, i0)
        a = halves(br)[0]
        add_to(a, fl)
        w.send(a, la, i0 + 4, right)
        w.wait(fr, i0 + 1)
        b = halves(bl)[1]
        add_to(b, fr)
        w.send(b, rb, i0 + 5, left)

    def third():
        a, b = halves(me)
        w.wait(lb, i0 + 2)
        w.wait(rb, i0 + 5)
        add_to(b, lb, rb)
        w.wait(ra, i0 + 3)
        w.wait(la, i0 + 4)
        add_to(a, la, ra)

    return [first, second, third]


def reduce_pairs(w, half, narrow, wide):
    c = w.c
    i0 = w.take(6)
    me, other = c.zl, 1 - c.zl

    def move(k, h, to, i, chip_id):
        w.send(half(k, h), to, i0 + i, chip_id)

    def got(k, h, ref, i):
        w.wait(ref, i0 + i)
        add_to(half(k, h), ref)

    def s0():
        move(c.kp, other, narrow(0), 0, c.zi)

    def s1():
        got(c.kp, me, narrow(0), 0)
        move(c.kp, me, narrow(1), 2, c.zo)
        move(c.kf, me, wide(0, me), 1, c.zi)

    def s2():
        got(c.kf, other, narrow(1), 2)
        move(c.kf, other, wide(0, other), 4, c.zi)

    def s3():
        got(c.ke, other, wide(0, other), 1)
        move(c.ke, other, wide(1, other), 3, c.zo)

    def s4():
        got(c.ke, me, wide(0, me), 4)
        move(c.ke, me, wide(1, me), 5, c.zo)

    def s5():
        got(c.zh, me, wide(1, me), 3)
        got(c.zh, other, wide(1, other), 5)

    return [s0, s1, s2, s3, s4, s5]


def reduce_relay(w, block, got, direct):
    c = w.c
    i0 = w.take(3)

    def send_all():
        for i, (k, to) in enumerate(((c.ke, c.zo), (c.kf, c.z2i), (c.kp, c.z3))):
            w.send(block(k), got[i], i0 + i, to)

    def wait_all():
        for i in range(3):
            w.wait(got[i], i0 + i)
        add_to(block(c.zh), *got)

    if direct:
        return [send_all, wait_all]

    def s0():
        w.send(block(c.kp), got[0], i0, c.zo)

    def s1():
        w.wait(got[0], i0)
        add_to(block(c.kf), got[0])
        w.send(block(c.kf), got[1], i0 + 1, c.zi)

    def s2():
        w.wait(got[1], i0 + 1)
        add_to(block(c.ke), got[1])
        w.send(block(c.ke), got[2], i0 + 2, c.zo)

    def s3():
        w.wait(got[2], i0 + 2)
        add_to(block(c.zh), got[2])

    return [s0, s1, s2, s3]


def reduce_events(c, w, r):
    G, events = r.G, {}

    def stage(st):
        dz, dx, dw = REDUCE.direct_z[st], REDUCE.direct_x[st], REDUCE.direct_wide[st]
        xa, xb = REDUCE.x(st)
        za, zb = REDUCE.z(st)
        nz = zb - za
        zm = (nz + 1) // 2

        def buf(name):
            return getattr(r, f"r{st}{name}")

        def sides(ref, cut):
            return [(ref.at[(i, slice(None), slice(0, cut))], ref.at[(i, slice(None), slice(cut, 2 * cut))]) for i in range(2)]

        bx, bxf, bxz = buf("x"), buf("xf"), buf("xz")
        x = chain(
            reduce_ring(
                w,
                lambda i: G.at[xa:xb, i],
                lambda i: (G.at[xa:xb, i, 0:2], G.at[xa:xb, i, 2:4]),
                sides(bx, 2),
                (bxf.at[0], bxf.at[1]),
                c.xr,
                c.xl,
                c.xo,
                c.x,
                [bx.at[i] for i in range(3)] if dw else None,
                dw,
            ),
            reduce_relay(w, lambda k: G.at[xa:xb, c.x, k], [bxz.at[i] for i in range(3)], dz),
        )
        bz, bzh, bzx = buf("z"), buf("zh"), buf("zx")
        z = chain(
            reduce_pairs(
                w,
                lambda k, h: G.at[za:zb, pl.ds(2 * h, 2), k],
                lambda i: bzh.at[i],
                lambda i, h: bz.at[i, :, pl.ds(2 * h, 2)],
            ),
            reduce_ring(
                w,
                lambda i: G.at[za:zb, i, c.zh],
                lambda i: (G.at[za : za + zm, i, c.zh], G.at[za + zm : zb, i, c.zh]),
                [(bzx.at[i, 0:zm], bzx.at[i, zm:nz]) for i in range(2)],
                (bzx.at[2, 0:zm], bzx.at[2, zm:nz]),
                c.xr,
                c.xl,
                c.xo,
                c.x,
                [bzx.at[i] for i in range(3)] if dx else None,
                dx,
            ),
        )
        mine = REDUCE.y(st, c.y)
        by, byf, byx, byxf, byz = buf("y"), buf("yf"), buf("yx"), buf("yxf"), buf("yz")
        y = chain(
            reduce_ring(
                w,
                lambda i: G.at[REDUCE.y(st, i)],
                lambda i: (G.at[REDUCE.y(st, i), 0:2], G.at[REDUCE.y(st, i), 2:4]),
                sides(by, 2),
                (byf.at[0], byf.at[1]),
                c.yr,
                c.yl,
                c.yo,
                c.y,
                [by.at[i] for i in range(3)] if dw else None,
                dw,
            ),
            reduce_ring(
                w,
                lambda i: G.at[mine, i],
                lambda i: (G.at[mine, i, 0:2], G.at[mine, i, 2:4]),
                sides(byx, 2),
                (byxf.at[0], byxf.at[1]),
                c.xr,
                c.xl,
                c.xo,
                c.x,
                [byx.at[i] for i in range(3)],
                True,
            ),
            reduce_relay(w, lambda k: G.at[mine, c.x, k], [byz.at[i] for i in range(3)], True),
        )

        def group(name, a, b):
            base = w.take(7)
            slab, held = buf("s" + name), buf("h" + name)

            def spread():
                row = lax.broadcasted_iota(jnp.int32, (64, 48), 0)
                col = lax.broadcasted_iota(jnp.int32, (64, 48), 1)
                pick = ((col // 6 == row // 8) & (col % 6 == row % 8)).astype(BF)
                for i in range(a, b):
                    o = dot(pick, G[REDUCE.tile(st, i, c.y), c.x, c.zh]).astype(BF)
                    slab[:, i - a] = o.reshape(8, 8, 128)
                for d in range(1, 8):
                    dm = (c.m + d) % 8
                    w.send(slab.at[dm], held.at[c.m], base + d - 1, c.f - c.m + dm)
                held[c.m] = slab[c.m]

            def collect():
                for d in range(1, 8):
                    w.wait(held.at[(c.m + 8 - d) % 8], base + d - 1)
                for i in range(a, b):
                    v = held[:, i - a].astype(F32)
                    if i < REDUCE.ny[st]:
                        for j in range(4):
                            r.done[c.s, REDUCE.tile(st, i, j)] = v[j] + v[j + 4]
                    else:
                        r.done[c.s, REDUCE.tile(st, i, 0)] = jnp.sum(v, axis=0)

            return [spread, collect]

        ny, nx = REDUCE.ny[st], REDUCE.nx[st]
        named(events, f"r{st}y", chain(y, group("y", 0, ny)))
        named(events, f"r{st}x", chain(x, group("x", ny, ny + nx)))
        named(events, f"r{st}z", chain(z, group("z", ny + nx, ny + nx + nz)))
        i0 = w.take(1)
        tiles = slice(REDUCE.first[st], REDUCE.first[st] + 4 * ny + nx + nz)

        def share():
            w.send(r.done.at[c.s, tiles], r.done.at[c.s, tiles], i0, {"seq": 1 - c.s})

        def shared():
            w.wait(r.done.at[1 - c.s, tiles], i0)

        named(events, f"r{st}d", [share, shared])

    for st in REDUCE.stages:
        stage(st)
    return events


def reduce_buffers():
    out = {}
    for st in REDUCE.stages:
        ny, nx, nz = REDUCE.ny[st], REDUCE.nx[st], REDUCE.nz[st]
        for name, dims in dict(
            x=(2 + REDUCE.direct_wide[st], nx, 4, 48, 128),
            xf=(2, nx, 2, 48, 128),
            xz=(3, nx, 48, 128),
            z=(2, nz, 4, 48, 128),
            zh=(2, nz, 2, 48, 128),
            zx=(3, nz, 48, 128),
            y=(2 + REDUCE.direct_wide[st], ny, 4, 4, 48, 128),
            yf=(2, ny, 2, 4, 48, 128),
            yx=(3, ny, 4, 48, 128),
            yxf=(2, ny, 2, 48, 128),
            yz=(3, ny, 48, 128),
            sx=(8, nx, 8, 128),
            hx=(8, nx, 8, 128),
            sy=(8, ny, 8, 128),
            hy=(8, ny, 8, 128),
            sz=(8, nz, 8, 128),
            hz=(8, nz, 8, 128),
        ).items():
            out[f"r{st}{name}"] = (dims, BF)
    return out


def rotary_table():
    freq = np.power(np.float32(10000.0), -2.0 * np.arange(32, dtype=np.float32) / np.float32(64))
    angle = np.arange(256, dtype=np.float32)[:, None] * freq.astype(np.float32)[None, :]
    cos, sin = np.cos(angle).astype(np.float32), np.sin(angle).astype(np.float32)
    terms = []
    for v in (np.concatenate([cos] * 4, axis=1), np.concatenate([-sin, sin] * 2, axis=1)):
        for _ in range(3):
            low = v.astype(BF)
            terms.append(low)
            v = v - low.astype(np.float32)
    return np.concatenate(terms, axis=1)


SCHEDULE = (
    77, 0, 1, 2, 97, 78, 3, 85, 90, 79, 98, 91, 80, 86, 105, 110, 99, 81, 106, 82, 87, 92, 111, 100, 88, 93, 94, 107,
    101, 112, 89, 83, 95, 102, 84, 113, 96, 4, 5, 114, 108, 6, 7, 8, 9, 10, 11, 12, 13, 14, 15, 16, 17, 109, 63, 103,
    115, 18, 104, 39, 116, 19, 20, 21, 22, 23, 24, 25, 26, 27, 28, 29, 30, 31, 32, 33, 34, 35, 36, 37, 38, 40, 41,
    42, 43, 44, 45, 123, 117, 130, 73, 46, 47, 48, 49, 50, 51, 52, 53, 54, 55, 56, 131, 57, 58, 59, 60, 61, 62, 64,
    65, 66, 118, 67, 68, 140, 153, 146, 124, 132, 133, 69, 70, 71, 72, 74, 154, 75, 141, 134, 147, 119, 125, 155,
    156, 76, 142, 157, 148, 126, 120, 135, 143, 149, 127, 144, 150, 158, 121, 136, 128, 122, 151, 137, 145, 159, 152,
    129, 138, 160, 161, 139, 162,
)

INPUTS = (
    "hidden", "d_out", "lengths", "source", "table", "qkv", "out", "up", "down",
    "gain_one", "gain_two", "down_bias", "up_bias",
)
OUTPUTS = ("output", "grad_hidden", "done")
BUFFERS = {
    "W": ((NT, 4, 4, 48, 128), BF),
    "G": ((NT, 4, 4, 48, 128), BF),
    **LAYER_BUFFERS,
    **gather_buffers(),
    **reduce_buffers(),
}
SEMS = 6 + 35 * len(GATHER.stages) + 58 * len(REDUCE.stages)


def step_kernel(*refs):
    r = Held()
    for name, ref in zip(INPUTS + OUTPUTS + tuple(BUFFERS), refs):
        setattr(r, name, ref)
    c = place()
    w = Wires(c, refs[-2], refs[-1])
    greeted = greet(c)
    events = {**layer_steps(c, w, r), **gather_events(c, w, r), **reduce_events(c, w, r)}
    fill_slab(c, r)
    events.pop("tables0")()
    pl.semaphore_wait(pltpu.get_barrier_semaphore(), greeted)
    steps = list(events.values())
    assert sorted(SCHEDULE) == list(range(len(steps)))
    for i in SCHEDULE:
        steps[i]()
    w.finish()


def finish_kernel(
    out_in, hidden_in, done, qkv, up, gain_one, gain_two, out, hidden, gqkv, gout, gup, gdown, g1, g2, gub, gdb
):
    out[...] = out_in[...]
    hidden[...] = hidden_in[...]
    for core in range(2):
        for i, t in enumerate(GQKV):
            n = (i // 3) * 768 + core * 384 + (i % 3) * 128
            gqkv[:, n : n + 128] = done[core, t, 0:6]
        for tiles, ref, half in ((GOUT, gout, 384), (GUP, gup, 1536), (GDOWN, gdown, 1536)):
            for i, t in enumerate(tiles):
                n = core * half + i * 128
                ref[:, n : n + 128] = done[core, t, 0:6]
    lane = lax.broadcasted_iota(jnp.int32, (6, 128), 1)
    row = lax.broadcasted_iota(jnp.int32, (6, 128), 0)
    one = done[0, GVEC, 0:6]
    both = one + done[1, GVEC, 0:6]

    def as_row(places):
        total = jnp.zeros((6, 128), F32)
        for v, at in places:
            total = jnp.where(lane == at, v, total)
        return jnp.sum(total, axis=0)

    def gain_grad(weight, grad, gain):
        return jnp.sum(weight[...].astype(F32) * grad[...], axis=1, keepdims=True) / column(gain, 1, 0)

    g1[...] = as_row([(gain_grad(qkv, gqkv, gain_one), row)])[0:6]
    g2[...] = as_row([(gain_grad(up, gup, gain_two), row)])[0:6]
    gdb[...] = as_row([(one[:, 2:3], row)])[0:6]
    gub[...] = as_row([(both[:, 4 + k : 5 + k], 4 * row + k) for k in range(4)])[0:24]


VM = pl.BlockSpec(memory_space=pltpu.VMEM)
LIMIT = 62 * 2**20


def shape(dims, dtype=F32):
    return jax.ShapeDtypeStruct(dims, dtype)


def per_device(
    hidden, d_out, lengths, slot_source, first_gain, qkv_weight, out_weight, second_gain, up_weight, up_bias,
    down_weight, down_bias,
):
    parts = pl.pallas_call(
        step_kernel,
        out_shape=(shape((256, 768), BF), shape((256, 768)), shape((2, NT, 8, 128))),
        in_specs=[VM, VM, pl.BlockSpec(memory_space=pltpu.SMEM)] + [VM] * 10,
        out_specs=(VM,) * 3,
        scratch_shapes=[pltpu.VMEM(*v) for v in BUFFERS.values()] + [pltpu.SemaphoreType.DMA((SEMS,))] * 2,
        compiler_params=pltpu.CompilerParams(collective_id=0, has_side_effects=True, vmem_limit_bytes=LIMIT),
    )(
        hidden[0], d_out[0], lengths, slot_source, rotary_table(),
        qkv_weight, out_weight.T, up_weight, down_weight.T,
        first_gain[None], second_gain[None], down_bias[None], up_bias[None],
    )
    output, grad_hidden, gqkv, gout, gup, gdown, g1, g2, gub, gdb = pl.pallas_call(
        finish_kernel,
        out_shape=(
            shape((256, 768), BF),
            shape((256, 768)),
            shape((6, 2304)),
            shape((6, 768)),
            shape((6, 3072)),
            shape((6, 3072)),
            shape((6,)),
            shape((6,)),
            shape((24,)),
            shape((6,)),
        ),
        in_specs=[VM] * 7,
        out_specs=(VM,) * 10,
    )(*parts, qkv_weight, up_weight, first_gain[None], second_gain[None])
    return (output[None], grad_hidden[None], g1, gqkv, gout.T, g2, gup, gub, gdown.T, gdb)


def solution(mesh):
    return jax.shard_map(
        per_device,
        mesh=mesh,
        in_specs=(
            P("fsdp", "seq", None),
            P("fsdp", "seq", None),
            P("fsdp", None),
            P("fsdp", None),
            P("fsdp"),
            P("fsdp", None),
            P(None, "fsdp"),
            P("fsdp"),
            P("fsdp", None),
            P("fsdp"),
            P(None, "fsdp"),
            P("fsdp"),
        ),
        out_specs=(
            P("fsdp", "seq", None),
            P("fsdp", "seq", None),
            P("fsdp"),
            P("fsdp", None),
            P(None, "fsdp"),
            P("fsdp"),
            P("fsdp", None),
            P("fsdp"),
            P(None, "fsdp"),
            P("fsdp"),
        ),
        check_vma=False,
    )
```
